256 devices in a mesh: replica: 16 (over y, z_lo), shard: 16 (over z_hi, x, core).
Axes of the slice: x: 4, y: 4, z: 8 (z_hi: 2, z_lo: 4; z = z_hi * 4 + z_lo), core: 2. Of those that a mesh axis runs over, the one named last changes fastest.
Arguments:
- outer_weight: float32 [16, 5120, 2048], P('replica', 'shard'), may hold values from -0.078125 to 0.078125
- inner_weight: bfloat16 [16, 5120, 2048], P('replica', 'shard'), may hold values from -0.078125 to 0.078125
- momentum: bfloat16 [16, 5120, 2048], P('replica', 'shard'), may hold values from -0.0390625 to 0.0390625
- matching: int32 [16], replicated, may hold values from 0 to 15, each once
- tokens: bfloat16 [16, 4096, 5120], P('replica', 'shard'), may hold values from -6 to 6
- norm_gain: float32 [16, 5120], P('replica'), may hold values from 0.1 to 1.9
- kv_bias: float32 [16, 2048], P('replica'), may hold values from -3 to 3
Outputs:
- new_outer: float32 [16, 5120, 2048], P('replica', 'shard')
- new_momentum: bfloat16 [16, 5120, 2048], P('replica', 'shard')
- keys_values: bfloat16 [16, 4096, 2048], P('replica', 'shard')
The draws below stay inside these ranges and needn't reach their ends.
Inputs may be any that keep to these rules, and one draw needn't show every extreme that they name: Replicas matching[2k] and matching[2k+1] are partners; every replica appears exactly once.
All inputs are finite; a program needn't handle non-finite values.
Results may differ from the reference program's by a relative error of at most 0.0074.
Values may be sent and summed in bfloat16 or wider, within the bound.
A program may use at most 128 MiB of HBM per device.

```python
import jax
import jax.numpy as jnp
from jax import lax

D = 5120
KV_HEADS = 8
HEAD_DIM = 128
TOKENS = 4096
KV = 2048
N_REPLICA = 16


def levels(own_key, extent, split, least, largest):
    level, own = 1.0, jax.random.fold_in(own_key, 6)
    for axis_at, shards_of in split:
        draws = jnp.exp(jax.random.uniform(jax.random.fold_in(own, axis_at), (shards_of,), jnp.float32, least / len(split), largest / len(split)))
        level = level * jnp.repeat(draws, extent[axis_at] // shards_of).reshape([-1 if axis == axis_at else 1 for axis in range(len(extent))])
    return level


def normal_values(rng, extent, width, bound, pieces=(), held_as=jnp.bfloat16):
    level = levels(rng, extent, pieces, -0.22, 0.18) if pieces else 1.0
    result = jax.random.normal(rng, extent, jnp.float32) * width * level
    return jnp.minimum(jnp.maximum(result, -bound), bound).astype(held_as)


def setup_inputs(seed: int = 0) -> dict:
    seeds = jax.random.split(jax.random.key(seed), 8)
    outer_weight = normal_values(seeds[0], (N_REPLICA, D, KV), D ** -0.5, 0.078125, ((0, 16), (1, 16)), jnp.float32)
    inner_weight = normal_values(seeds[1], (N_REPLICA, D, KV), D ** -0.5, 0.078125, ((0, 16), (1, 16)))
    momentum = normal_values(seeds[2], (N_REPLICA, D, KV), (4 * D) ** -0.5, 0.0390625, ((0, 16), (1, 16)))
    matching = jax.random.permutation(seeds[3], N_REPLICA).astype(jnp.int32)
    tokens = normal_values(seeds[4], (N_REPLICA, TOKENS, D), 1.0, 6.0, ((0, 16), (1, 16)))
    norm_gain = jnp.clip(1.0 + 0.18 * jax.random.normal(seeds[5], (N_REPLICA, D), jnp.float32), 0.1, 1.9)
    kv_bias = normal_values(seeds[6], (N_REPLICA, KV), 0.5, 3.0, ((0, 16),), jnp.float32)
    return {"outer_weight": outer_weight, "inner_weight": inner_weight, "momentum": momentum, "matching": matching, "tokens": tokens, "norm_gain": norm_gain, "kv_bias": kv_bias}


momentum_rate = 0.9
outer_rate = 0.7
gossip_rate = 0.5
norm_eps = 1e-06
rope_base = 1000000.0

def partner_table(matching):
    total_count = matching.shape[0]
    indices = jnp.arange(total_count, dtype=jnp.int32)
    matches = (matching[None, :] == indices[:, None]).astype(jnp.int32)
    position = lax.optimization_barrier(jnp.sum(matches * indices[None, :], axis=1)).astype(jnp.int32)
    mate_pos = position + 1 - 2 * (position % 2)
    picked = (indices[None, :] == mate_pos[:, None]).astype(jnp.int32)
    return lax.optimization_barrier(jnp.sum(picked * matching[None, :], axis=1)).astype(jnp.int32)

def rounded(values):
    return lax.optimization_barrier(values.astype(jnp.bfloat16)).astype(jnp.float32)

def rms_normed(token_rows, gain):
    values = token_rows.astype(jnp.float32)
    mean_square = lax.optimization_barrier(jnp.mean(values * values, axis=-1, keepdims=True))
    return (values * lax.rsqrt(mean_square + norm_eps) * gain[None, :]).astype(jnp.bfloat16)

def rotary(projected, positions):
    tok_count = projected.shape[0]
    key_width = KV_HEADS * HEAD_DIM
    half_dim = HEAD_DIM // 2
    exponents = jnp.arange(half_dim, dtype=jnp.float32) * (2.0 / HEAD_DIM)
    inverse = rope_base ** (-exponents)
    angles = positions[:, None] * inverse[None, :]
    cosine = jnp.cos(angles)[:, None, :]
    sine_vals = jnp.sin(angles)[:, None, :]
    key_cols = projected[:, :key_width].reshape(tok_count, KV_HEADS, HEAD_DIM)
    first_half = key_cols[..., :half_dim]
    second_half = key_cols[..., half_dim:]
    turned = jnp.concatenate([first_half * cosine - second_half * sine_vals, second_half * cosine + first_half * sine_vals], axis=-1)
    return jnp.concatenate([turned.reshape(tok_count, key_width), projected[:, key_width:]], axis=1)

def reference(outer_weight, inner_weight, momentum, matching, tokens, norm_gain, kv_bias):
    partner = partner_table(matching)
    positions = jnp.arange(tokens.shape[1], dtype=jnp.int32).astype(jnp.float32)

    def per_replica(replica_id):
        mate_id = partner[replica_id]
        own_outer = outer_weight[replica_id]
        mate_outer = outer_weight[mate_id]
        own_delta = rounded(own_outer - inner_weight[replica_id].astype(jnp.float32))
        mate_delta = rounded(mate_outer - inner_weight[mate_id].astype(jnp.float32))
        pair_delta = rounded((own_delta + mate_delta) * 0.5)
        pair_outer = rounded((rounded(own_outer) + rounded(mate_outer)) * 0.5)
        velocity = momentum_rate * momentum[replica_id].astype(jnp.float32) + pair_delta
        updated = own_outer - outer_rate * (pair_delta + momentum_rate * velocity) - gossip_rate * (own_outer - pair_outer)
        normed = rms_normed(tokens[replica_id], norm_gain[replica_id])
        projected = jnp.dot(normed, updated.astype(jnp.bfloat16), preferred_element_type=jnp.float32) + kv_bias[replica_id][None, :]
        return (updated, velocity.astype(jnp.bfloat16), rotary(projected, positions).astype(jnp.bfloat16))
    new_outer, new_momentum, keys_values = lax.map(per_replica, jnp.arange(N_REPLICA, dtype=jnp.int32))
    return (new_outer, new_momentum, keys_values)
```

```python
import functools

import jax
import jax.numpy as jnp
from jax import lax
from jax.experimental import pallas as pl
from jax.experimental.pallas import tpu as pltpu
from jax.sharding import PartitionSpec as P

MESH = pl.DeviceIdType.MESH
BF16 = jnp.bfloat16
F32 = jnp.float32

HEAD_DIM = 128
KEY_WIDTH = 1024
momentum_rate = 0.9
outer_rate = 0.7
gossip_rate = 0.5
norm_eps = 1e-06
rope_base = 1000000.0

ROWS = 320
WIDTH = 2048
TOKENS = 256
DEPTH = 5120
GROUP = ROWS // 4
HALF = ROWS // 2
CHUNKS = 8
CW = WIDTH // CHUNKS
AHEAD = 2
NORM_TICKS = 4

A, B, C, D, X1, X2, F1, F2, K = range(9)
SA, SB, SC, SW = range(4)
LO, LI, OO, OM, OK = range(5)


def kernel(
    slots,
    mate_ref,
    outer_hbm,
    inner_hbm,
    moment_hbm,
    token_hbm,
    gain_ref,
    bias_ref,
    cos_ref,
    sin_ref,
    new_outer_hbm,
    new_moment_hbm,
    kv_hbm,
    outer,
    inner,
    moment,
    normed,
    sent,
    pool,
    crossing,
    means,
    pair,
    weights,
    kv,
    recv,
    send,
    local,
    single,
):
    r, s = lax.axis_index("replica"), lax.axis_index("shard")
    y, zl = r // 4, r % 4
    zh, x, core = s // 8, (s // 2) % 4, s % 2
    side = zl // 2
    hub_z = 1 + side
    is_hub = zl == hub_z
    far = 3 - zl
    edge = 3 * side

    def place(py, pz, ph, px, pc):
        return (py * 4 + pz, ph * 8 + px * 2 + pc)

    right, left = (x + 1) % 4, (x + 3) % 4
    to_core = place(y, zl, zh, x, 1 - core)
    to_right = place(y, zl, zh, right, core)
    to_left = place(y, zl, zh, left, core)
    to_far = place(y, zl, 1 - zh, x, core)

    def rows_of(ph, px, pc, start=0, size=ROWS):
        return pl.ds(pl.multiple_of((ph * 8 + px * 2 + pc) * ROWS + start, 16), size)

    def cols(n):
        return pl.ds(pl.multiple_of(n * CW, CW), CW)

    def remote(src, dst, ssem, rsem, device):
        pltpu.make_async_remote_copy(
            src_ref=src, dst_ref=dst, send_sem=ssem, recv_sem=rsem, device_id=device, device_id_type=MESH
        ).start()

    def taken(ref, sem):
        pltpu.make_async_copy(ref, ref, sem).wait()

    def loads(n):
        return (
            pltpu.make_async_copy(outer_hbm.at[:, cols(n)], outer.at[n], local.at[LO, n]),
            pltpu.make_async_copy(inner_hbm.at[:, cols(n)], inner.at[n], local.at[LI, n]),
        )

    def moment_load(n):
        return pltpu.make_async_copy(moment_hbm.at[:, cols(n)], moment.at[n], local.at[OM, n])

    token_load = pltpu.make_async_copy(token_hbm, normed, single.at[0])

    def start_loads(n, _):
        for copy in loads(n):
            copy.start()
        return 0

    lax.fori_loop(0, CHUNKS, start_loads, 0)
    token_load.start()

    def start_moment(n, _):
        moment_load(n).start()
        return 0

    lax.fori_loop(0, CHUNKS, start_moment, 0)

    barrier = pltpu.get_barrier_semaphore()

    def greet(device):
        pl.semaphore_signal(barrier, inc=1, device_id=device, device_id_type=MESH)

    for device in (to_core, to_right, to_left, to_far):
        greet(device)

    @pl.when(is_hub)
    def _():
        for step in range(4):
            greet(place((y + step) % 4, edge, zh, x, core))
        for step in range(1, 4):
            greet(place((y + step) % 4, zl, zh, x, core))
        greet(place(y, far, zh, x, core))
        pl.semaphore_wait(barrier, 12)

    @pl.when(jnp.logical_not(is_hub))
    def _():
        for step in range(4):
            greet(place((y + step) % 4, hub_z, zh, x, core))
        pl.semaphore_wait(barrier, 8)

    item = (zl % 2) * 4 + y

    def send_rows(n):
        for copy in loads(n):
            copy.wait()

        def group(g, _):
            rows = pl.ds(pl.multiple_of(g * GROUP, 16), GROUP)
            own = outer[n, rows, :]
            sent[n, g, 0] = (own - inner[n, rows, :].astype(F32)).astype(BF16)
            sent[n, g, 1] = own.astype(BF16)
            return 0

        lax.fori_loop(0, 4, group, 0)
        for step in range(4):
            to_y = (y + step) % 4
            src, dst = sent.at[n, to_y], pool.at[n, item]
            if step:
                remote(src, dst, send.at[SA, n], recv.at[A, n], place(to_y, hub_z, zh, x, core))
            else:

                @pl.when(is_hub)
                def _():
                    pltpu.make_async_copy(src, dst, recv.at[A, n]).start()

                @pl.when(jnp.logical_not(is_hub))
                def _():
                    remote(src, dst, send.at[SA, n], recv.at[A, n], place(to_y, hub_z, zh, x, core))

    def swap_sides(n):
        taken(pool.at[n, pl.ds(0, 8)], recv.at[A, n])
        if slots < 8:

            def part(i, _):
                v = i // 5
                rows = pl.ds(pl.multiple_of((i % 5) * 16, 16), 16)
                held = [pool[n, j, v, rows, :] for j in range(8)]
                for k in range(slots):
                    which = mate_ref[16 + side * 8 + k]
                    value = held[0]
                    for j in range(1, 8):
                        value = jnp.where(which == j, held[j], value)
                    crossing[n, k, v, rows, :] = value
                return 0

            lax.fori_loop(0, 10, part, 0)
            src = crossing.at[n]
        else:
            src = pool.at[n, pl.ds(0, 8)]
        remote(src, pool.at[n, pl.ds(8, slots)], send.at[SB, n], recv.at[B, n], place(y, far, zh, x, core))

    def average(n):
        taken(pool.at[n, pl.ds(8, slots)], recv.at[B, n])
        mates = [mate_ref[side * 8 + k] for k in range(8)]

        def part(i, _):
            v = i // 5
            rows = pl.ds(pl.multiple_of((i % 5) * 16, 16), 16)
            held = [pool[n, j, v, rows, :] for j in range(8 + slots)]
            for k in range(8):
                value = held[0]
                for j in range(1, 8 + slots):
                    value = jnp.where(mates[k] == j, held[j], value)
                means[n, k, v, rows, :] = ((held[k].astype(F32) + value.astype(F32)) * 0.5).astype(BF16)
            return 0

        lax.fori_loop(0, 10, part, 0)
        for step in range(4):
            to_y = (y + step) % 4
            src, dst = means.at[n, (zl % 2) * 4 + to_y], pair.at[n, y]
            if step:
                remote(src, dst, send.at[SC, n], recv.at[C, n], place(to_y, zl, zh, x, core))
            else:
                pltpu.make_async_copy(src, dst, recv.at[C, n]).start()
            remote(
                means.at[n, (edge % 2) * 4 + to_y],
                dst,
                send.at[SC, n],
                recv.at[C, n],
                place(to_y, edge, zh, x, core),
            )

    def pass_on(n, rows, rsem, device):
        block = weights.at[n, rows]
        remote(block, block, send.at[SW, n], recv.at[rsem, n], device)

    def update(n):
        taken(pair.at[n], recv.at[C, n])
        moment_load(n).wait()

        def group(g, _):
            rows = pl.ds(pl.multiple_of(g * GROUP, 16), GROUP)
            own = outer[n, rows, :]
            delta = pair[n, g, 0].astype(F32)
            velocity = momentum_rate * moment[n, rows, :].astype(F32) + delta
            updated = (
                own
                - outer_rate * (delta + momentum_rate * velocity)
                - gossip_rate * (own - pair[n, g, 1].astype(F32))
            )
            outer[n, rows, :] = updated
            moment[n, rows, :] = velocity.astype(BF16)
            weights[n, pl.ds(pl.multiple_of(s * ROWS + g * GROUP, 16), GROUP), :] = updated.astype(BF16)
            return 0

        lax.fori_loop(0, 4, group, 0)
        own_rows = rows_of(zh, x, core)
        pass_on(n, own_rows, D, to_far)
        pass_on(n, own_rows, X1, to_right)
        pass_on(n, own_rows, X1, to_left)
        pass_on(n, own_rows, K, to_core)
        outer_store(n).start()
        moment_store(n).start()

    def outer_store(n):
        return pltpu.make_async_copy(outer.at[n], new_outer_hbm.at[:, cols(n)], local.at[OO, n])

    def moment_store(n):
        return pltpu.make_async_copy(moment.at[n], new_moment_hbm.at[:, cols(n)], local.at[OM, n])

    def kv_store(n):
        return pltpu.make_async_copy(kv.at[n], kv_hbm.at[:, cols(n)], local.at[OK, n])

    def forward(n, ph, rsem):
        pass_on(n, rows_of(ph, left, core, 0, HALF), rsem, to_right)
        pass_on(n, rows_of(ph, right, core, HALF, HALF), rsem, to_left)
        pass_on(n, rows_of(ph, left, core), K, to_core)
        pass_on(n, rows_of(ph, right, core), K, to_core)

    def first_hop(n):
        taken(weights.at[n, rows_of(1 - zh, x, core)], recv.at[D, n])
        far_rows = rows_of(1 - zh, x, core)
        pass_on(n, far_rows, X2, to_right)
        pass_on(n, far_rows, X2, to_left)
        pass_on(n, far_rows, K, to_core)
        taken(weights.at[n, pl.ds(0, 2 * ROWS)], recv.at[X1, n])
        forward(n, zh, F1)

    def second_hop(n):
        taken(weights.at[n, pl.ds(0, 2 * ROWS)], recv.at[X2, n])
        forward(n, 1 - zh, F2)
        taken(weights.at[n, pl.ds(0, ROWS)], recv.at[F1, n])
        pass_on(n, rows_of(zh, (x + 2) % 4, core), K, to_core)

    def third_hop(n):
        taken(weights.at[n, pl.ds(0, ROWS)], recv.at[F2, n])
        pass_on(n, rows_of(1 - zh, (x + 2) % 4, core), K, to_core)

    def norm_rows(t):
        @pl.when(t == 0)
        def _():
            token_load.wait()

        per_tick = TOKENS // NORM_TICKS

        def part(i, _):
            rows = pl.ds(pl.multiple_of(t * per_tick + i * 16, 16), 16)
            values = normed[rows, :].astype(F32)
            mean_square = jnp.mean(values * values, axis=-1, keepdims=True)
            normed[rows, :] = (values * lax.rsqrt(mean_square + norm_eps) * gain_ref[...]).astype(BF16)
            return 0

        lax.fori_loop(0, per_tick // 16, part, 0)

    def project(n):
        taken(weights.at[n, pl.ds(0, DEPTH // 2)], recv.at[K, n])
        out = jnp.dot(normed[...], weights[n], preferred_element_type=F32) + bias_ref[:, cols(n)]

        @pl.when(n * CW < KEY_WIDTH)
        def _():
            for h in range(CW // HEAD_DIM):
                head = out[:, h * HEAD_DIM : (h + 1) * HEAD_DIM]
                turned = head * cos_ref[...] + pltpu.roll(head, HEAD_DIM // 2, 1) * sin_ref[...]
                kv[n, :, h * HEAD_DIM : (h + 1) * HEAD_DIM] = turned.astype(BF16)

        @pl.when(n * CW >= KEY_WIDTH)
        def _():
            kv[n] = out.astype(BF16)

        kv_store(n).start()

    def first_rows(n, _):
        send_rows(n)
        return 0

    lax.fori_loop(0, AHEAD, first_rows, 0)

    def tick(t, _):
        @pl.when(t + AHEAD < CHUNKS)
        def _():
            send_rows(t + AHEAD)

        @pl.when(jnp.logical_and(is_hub, t < CHUNKS))
        def _():
            swap_sides(t)

        @pl.when(t < NORM_TICKS)
        def _():
            norm_rows(t)

        def staged(lag, stage, also=None):
            ready = jnp.logical_and(t >= lag, t < CHUNKS + lag)

            @pl.when(ready if also is None else jnp.logical_and(ready, also))
            def _():
                stage(t - lag)

        staged(1, average, is_hub)
        staged(2, update)
        staged(3, first_hop)
        staged(4, second_hop)
        staged(5, third_hop)
        staged(6, project)
        return 0

    lax.fori_loop(0, CHUNKS + 6, tick, 0)

    def drain(n, _):
        @pl.when(is_hub)
        def _():
            taken(sent.at[n, pl.ds(0, 3)], send.at[SA, n])
            taken(pool.at[n, pl.ds(8, slots)], send.at[SB, n])
            taken(means.at[n, pl.ds(0, 7)], send.at[SC, n])

        @pl.when(jnp.logical_not(is_hub))
        def _():
            taken(sent.at[n], send.at[SA, n])

        taken(weights.at[n, pl.ds(0, 15 * ROWS)], send.at[SW, n])
        outer_store(n).wait()
        moment_store(n).wait()
        kv_store(n).wait()
        return 0

    lax.fori_loop(0, CHUNKS, drain, 0)


def partner_table(matching):
    total_count = matching.shape[0]
    indices = jnp.arange(total_count, dtype=jnp.int32)
    matches = (matching[None, :] == indices[:, None]).astype(jnp.int32)
    position = jnp.sum(matches * indices[None, :], axis=1)
    mate_pos = position + 1 - 2 * (position % 2)
    picked = (indices[None, :] == mate_pos[:, None]).astype(jnp.int32)
    return jnp.sum(picked * matching[None, :], axis=1)


def on_device(outer_weight, inner_weight, momentum, matching, tokens, norm_gain, kv_bias):
    partner = partner_table(matching)
    order = jnp.arange(16, dtype=jnp.int32)
    replica_of = (order % 4) * 4 + (order // 8) * 2 + (order // 4) % 2
    mate = jnp.sum(jnp.where(replica_of[:, None] == jnp.arange(16)[None, :], partner[None, :], 0), axis=1)
    mate_item = (mate % 4) // 2 * 8 + (mate % 2) * 4 + mate // 4
    same_side = mate_item // 8 == order // 8
    table = jnp.where(same_side, mate_item % 8, 8 + mate_item % 8).astype(jnp.int32)

    positions = (lax.axis_index("shard") * TOKENS + jnp.arange(TOKENS, dtype=jnp.int32)).astype(F32)
    exponents = jnp.arange(HEAD_DIM // 2, dtype=F32) * (2.0 / HEAD_DIM)
    angles = positions[:, None] * (rope_base ** (-exponents))[None, :]
    cosine, sine = jnp.cos(angles), jnp.sin(angles)
    cosine = jnp.concatenate([cosine, cosine], axis=1)
    sine = jnp.concatenate([-sine, sine], axis=1)

    slots = 8
    hbm = pl.BlockSpec(memory_space=pl.ANY)
    vmem = pl.BlockSpec(memory_space=pltpu.VMEM)
    smem = pl.BlockSpec(memory_space=pltpu.SMEM)
    new_outer, new_moment, kv = pl.pallas_call(
        functools.partial(kernel, slots),
        out_shape=(
            jax.ShapeDtypeStruct((ROWS, WIDTH), F32),
            jax.ShapeDtypeStruct((ROWS, WIDTH), BF16),
            jax.ShapeDtypeStruct((TOKENS, WIDTH), BF16),
        ),
        in_specs=[smem, hbm, hbm, hbm, hbm, vmem, vmem, vmem, vmem],
        out_specs=(hbm, hbm, hbm),
        scratch_shapes=[
            pltpu.VMEM((CHUNKS, ROWS, CW), F32),
            pltpu.VMEM((CHUNKS, ROWS, CW), BF16),
            pltpu.VMEM((CHUNKS, ROWS, CW), BF16),
            pltpu.VMEM((TOKENS, DEPTH), BF16),
            pltpu.VMEM((CHUNKS, 4, 2, GROUP, CW), BF16),
            pltpu.VMEM((CHUNKS, 8 + slots, 2, GROUP, CW), BF16),
            pltpu.VMEM((CHUNKS if slots < 8 else 1, slots, 2, GROUP, CW), BF16),
            pltpu.VMEM((CHUNKS, 8, 2, GROUP, CW), BF16),
            pltpu.VMEM((CHUNKS, 4, 2, GROUP, CW), BF16),
            pltpu.VMEM((CHUNKS, DEPTH, CW), BF16),
            pltpu.VMEM((CHUNKS, TOKENS, CW), BF16),
            pltpu.SemaphoreType.DMA((9, CHUNKS)),
            pltpu.SemaphoreType.DMA((4, CHUNKS)),
            pltpu.SemaphoreType.DMA((5, CHUNKS)),
            pltpu.SemaphoreType.DMA((1,)),
        ],
        compiler_params=pltpu.CompilerParams(
            collective_id=0, has_side_effects=True, vmem_limit_bytes=62 * 2**20
        ),
    )(
        table,
        outer_weight[0],
        inner_weight[0],
        momentum[0],
        tokens[0],
        norm_gain,
        kv_bias,
        cosine,
        sine,
    )
    return (new_outer[None], new_moment[None], kv[None])


def solution(mesh):
    in_specs = (
        P("replica", "shard", None),
        P("replica", "shard", None),
        P("replica", "shard", None),
        P(),
        P("replica", "shard", None),
        P("replica", None),
        P("replica", None),
    )
    out_specs = (
        P("replica", "shard", None),
        P("replica", "shard", None),
        P("replica", "shard", None),
    )
    return jax.shard_map(on_device, mesh=mesh, in_specs=in_specs, out_specs=out_specs, check_vma=False)
```

```python
import functools

import jax
import jax.numpy as jnp
from jax import lax
from jax.experimental import pallas as pl
from jax.experimental.pallas import tpu as pltpu
from jax.sharding import PartitionSpec as P

MESH = pl.DeviceIdType.MESH
BF16 = jnp.bfloat16
F32 = jnp.float32

HEAD_DIM = 128
KEY_WIDTH = 1024
momentum_rate = 0.9
outer_rate = 0.7
gossip_rate = 0.5
norm_eps = 1e-06
rope_base = 1000000.0

ROWS = 320
WIDTH = 2048
TOKENS = 256
DEPTH = 5120
GROUP = ROWS // 4
HALF = ROWS // 2
CHUNKS = 8
CW = WIDTH // CHUNKS
AHEAD = 2
NORM_TICKS = 4

A, B, C, D, X1, X2, F1, F2, K = range(9)
SA, SB, SC, SW = range(4)
LO, LI, OO, OM, OK = range(5)


def kernel(
    slots,
    mate_ref,
    outer_hbm,
    inner_hbm,
    moment_hbm,
    token_hbm,
    gain_ref,
    bias_ref,
    cos_ref,
    sin_ref,
    new_outer_hbm,
    new_moment_hbm,
    kv_hbm,
    outer,
    inner,
    moment,
    normed,
    sent,
    pool,
    crossing,
    means,
    pair,
    weights,
    kv,
    recv,
    send,
    local,
    single,
):
    r, s = lax.axis_index("replica"), lax.axis_index("shard")
    y, zl = r // 4, r % 4
    zh, x, core = s // 8, (s // 2) % 4, s % 2
    side = zl // 2
    hub_z = 1 + side
    is_hub = zl == hub_z
    far = 3 - zl
    edge = 3 * side

    def place(py, pz, ph, px, pc):
        return (py * 4 + pz, ph * 8 + px * 2 + pc)

    right, left = (x + 1) % 4, (x + 3) % 4
    to_core = place(y, zl, zh, x, 1 - core)
    to_right = place(y, zl, zh, right, core)
    to_left = place(y, zl, zh, left, core)
    to_far = place(y, zl, 1 - zh, x, core)

    def rows_of(ph, px, pc, start=0, size=ROWS):
        return pl.ds(pl.multiple_of((ph * 8 + px * 2 + pc) * ROWS + start, 16), size)

    def cols(n):
        return pl.ds(pl.multiple_of(n * CW, CW), CW)

    def remote(src, dst, ssem, rsem, device):
        pltpu.make_async_remote_copy(
            src_ref=src, dst_ref=dst, send_sem=ssem, recv_sem=rsem, device_id=device, device_id_type=MESH
        ).start()

    def taken(ref, sem):
        pltpu.make_async_copy(ref, ref, sem).wait()

    def loads(n):
        return (
            pltpu.make_async_copy(outer_hbm.at[:, cols(n)], outer.at[n], local.at[LO, n]),
            pltpu.make_async_copy(inner_hbm.at[:, cols(n)], inner.at[n], local.at[LI, n]),
        )

    def moment_load(n):
        return pltpu.make_async_copy(moment_hbm.at[:, cols(n)], moment.at[n], local.at[OM, n])

    token_load = pltpu.make_async_copy(token_hbm, normed, single.at[0])

    def start_loads(n, _):
        for copy in loads(n):
            copy.start()
        return 0

    lax.fori_loop(0, CHUNKS, start_loads, 0)
    token_load.start()

    def start_moment(n, _):
        moment_load(n).start()
        return 0

    lax.fori_loop(0, CHUNKS, start_moment, 0)

    barrier = pltpu.get_barrier_semaphore()

    def greet(device):
        pl.semaphore_signal(barrier, inc=1, device_id=device, device_id_type=MESH)

    for device in (to_core, to_right, to_left, to_far):
        greet(device)

    @pl.when(is_hub)
    def _():
        for step in range(4):
            greet(place((y + step) % 4, edge, zh, x, core))
        for step in range(1, 4):
            greet(place((y + step) % 4, zl, zh, x, core))
        greet(place(y, far, zh, x, core))
        pl.semaphore_wait(barrier, 12)

    @pl.when(jnp.logical_not(is_hub))
    def _():
        for step in range(4):
            greet(place((y + step) % 4, hub_z, zh, x, core))
        pl.semaphore_wait(barrier, 8)

    item = (zl % 2) * 4 + y

    def send_rows(n):
        for copy in loads(n):
            copy.wait()

        def group(g, _):
            rows = pl.ds(pl.multiple_of(g * GROUP, 16), GROUP)
            own = outer[n, rows, :]
            sent[n, g, 0] = (own - inner[n, rows, :].astype(F32)).astype(BF16)
            sent[n, g, 1] = own.astype(BF16)
            return 0

        lax.fori_loop(0, 4, group, 0)
        for step in range(4):
            to_y = (y + step) % 4
            src, dst = sent.at[n, to_y], pool.at[n, item]
            if step:
                remote(src, dst, send.at[SA, n], recv.at[A, n], place(to_y, hub_z, zh, x, core))
            else:

                @pl.when(is_hub)
                def _():
                    pltpu.make_async_copy(src, dst, recv.at[A, n]).start()

                @pl.when(jnp.logical_not(is_hub))
                def _():
                    remote(src, dst, send.at[SA, n], recv.at[A, n], place(to_y, hub_z, zh, x, core))

    def swap_sides(n):
        taken(pool.at[n, pl.ds(0, 8)], recv.at[A, n])
        if slots < 8:

            def part(i, _):
                v = i // 5
                rows = pl.ds(pl.multiple_of((i % 5) * 16, 16), 16)
                held = [pool[n, j, v, rows, :] for j in range(8)]
                for k in range(slots):
                    which = mate_ref[16 + side * 8 + k]
                    value = held[0]
                    for j in range(1, 8):
                        value = jnp.where(which == j, held[j], value)
                    crossing[n, k, v, rows, :] = value
                return 0

            lax.fori_loop(0, 10, part, 0)
            src = crossing.at[n]
        else:
            src = pool.at[n, pl.ds(0, 8)]
        remote(src, pool.at[n, pl.ds(8, slots)], send.at[SB, n], recv.at[B, n], place(y, far, zh, x, core))

    def average(n):
        taken(pool.at[n, pl.ds(8, slots)], recv.at[B, n])
        first = side * 8 + (0 if slots < 8 else 32)
        mates = [mate_ref[first + k] for k in range(8)]

        def part(i, _):
            v = i // 5
            rows = pl.ds(pl.multiple_of((i % 5) * 16, 16), 16)
            held = [pool[n, j, v, rows, :] for j in range(8 + slots)]
            for k in range(8):
                value = held[0]
                for j in range(1, 8 + slots):
                    value = jnp.where(mates[k] == j, held[j], value)
                means[n, k, v, rows, :] = ((held[k].astype(F32) + value.astype(F32)) * 0.5).astype(BF16)
            return 0

        lax.fori_loop(0, 10, part, 0)
        for step in range(4):
            to_y = (y + step) % 4
            src, dst = means.at[n, (zl % 2) * 4 + to_y], pair.at[n, y]
            if step:
                remote(src, dst, send.at[SC, n], recv.at[C, n], place(to_y, zl, zh, x, core))
            else:
                pltpu.make_async_copy(src, dst, recv.at[C, n]).start()
            remote(
                means.at[n, (edge % 2) * 4 + to_y],
                dst,
                send.at[SC, n],
                recv.at[C, n],
                place(to_y, edge, zh, x, core),
            )

    def pass_on(n, rows, rsem, device):
        block = weights.at[n, rows]
        remote(block, block, send.at[SW, n], recv.at[rsem, n], device)

    def update(n):
        taken(pair.at[n], recv.at[C, n])
        moment_load(n).wait()

        def group(g, _):
            rows = pl.ds(pl.multiple_of(g * GROUP, 16), GROUP)
            own = outer[n, rows, :]
            delta = pair[n, g, 0].astype(F32)
            velocity = momentum_rate * moment[n, rows, :].astype(F32) + delta
            updated = (
                own
                - outer_rate * (delta + momentum_rate * velocity)
                - gossip_rate * (own - pair[n, g, 1].astype(F32))
            )
            outer[n, rows, :] = updated
            moment[n, rows, :] = velocity.astype(BF16)
            weights[n, pl.ds(pl.multiple_of(s * ROWS + g * GROUP, 16), GROUP), :] = updated.astype(BF16)
            return 0

        lax.fori_loop(0, 4, group, 0)
        own_rows = rows_of(zh, x, core)
        pass_on(n, own_rows, D, to_far)
        pass_on(n, own_rows, X1, to_right)
        pass_on(n, own_rows, X1, to_left)
        pass_on(n, own_rows, K, to_core)
        outer_store(n).start()
        moment_store(n).start()

    def outer_store(n):
        return pltpu.make_async_copy(outer.at[n], new_outer_hbm.at[:, cols(n)], local.at[OO, n])

    def moment_store(n):
        return pltpu.make_async_copy(moment.at[n], new_moment_hbm.at[:, cols(n)], local.at[OM, n])

    def kv_store(n):
        return pltpu.make_async_copy(kv.at[n], kv_hbm.at[:, cols(n)], local.at[OK, n])

    def forward(n, ph, rsem):
        pass_on(n, rows_of(ph, left, core, 0, HALF), rsem, to_right)
        pass_on(n, rows_of(ph, right, core, HALF, HALF), rsem, to_left)
        pass_on(n, rows_of(ph, left, core), K, to_core)
        pass_on(n, rows_of(ph, right, core), K, to_core)

    def first_hop(n):
        taken(weights.at[n, rows_of(1 - zh, x, core)], recv.at[D, n])
        far_rows = rows_of(1 - zh, x, core)
        pass_on(n, far_rows, X2, to_right)
        pass_on(n, far_rows, X2, to_left)
        pass_on(n, far_rows, K, to_core)
        taken(weights.at[n, pl.ds(0, 2 * ROWS)], recv.at[X1, n])
        forward(n, zh, F1)

    def second_hop(n):
        taken(weights.at[n, pl.ds(0, 2 * ROWS)], recv.at[X2, n])
        forward(n, 1 - zh, F2)
        taken(weights.at[n, pl.ds(0, ROWS)], recv.at[F1, n])
        pass_on(n, rows_of(zh, (x + 2) % 4, core), K, to_core)

    def third_hop(n):
        taken(weights.at[n, pl.ds(0, ROWS)], recv.at[F2, n])
        pass_on(n, rows_of(1 - zh, (x + 2) % 4, core), K, to_core)

    def norm_rows(t):
        @pl.when(t == 0)
        def _():
            token_load.wait()

        per_tick = TOKENS // NORM_TICKS

        def part(i, _):
            rows = pl.ds(pl.multiple_of(t * per_tick + i * 16, 16), 16)
            values = normed[rows, :].astype(F32)
            mean_square = jnp.mean(values * values, axis=-1, keepdims=True)
            normed[rows, :] = (values * lax.rsqrt(mean_square + norm_eps) * gain_ref[...]).astype(BF16)
            return 0

        lax.fori_loop(0, per_tick // 16, part, 0)

    def project(n):
        taken(weights.at[n, pl.ds(0, DEPTH // 2)], recv.at[K, n])
        out = jnp.dot(normed[...], weights[n], preferred_element_type=F32) + bias_ref[:, cols(n)]

        @pl.when(n * CW < KEY_WIDTH)
        def _():
            for h in range(CW // HEAD_DIM):
                head = out[:, h * HEAD_DIM : (h + 1) * HEAD_DIM]
                turned = head * cos_ref[...] + pltpu.roll(head, HEAD_DIM // 2, 1) * sin_ref[...]
                kv[n, :, h * HEAD_DIM : (h + 1) * HEAD_DIM] = turned.astype(BF16)

        @pl.when(n * CW >= KEY_WIDTH)
        def _():
            kv[n] = out.astype(BF16)

        kv_store(n).start()

    def first_rows(n, _):
        send_rows(n)
        return 0

    lax.fori_loop(0, AHEAD, first_rows, 0)

    def tick(t, _):
        @pl.when(t + AHEAD < CHUNKS)
        def _():
            send_rows(t + AHEAD)

        @pl.when(jnp.logical_and(is_hub, t < CHUNKS))
        def _():
            swap_sides(t)

        @pl.when(t < NORM_TICKS)
        def _():
            norm_rows(t)

        def staged(lag, stage, also=None):
            ready = jnp.logical_and(t >= lag, t < CHUNKS + lag)

            @pl.when(ready if also is None else jnp.logical_and(ready, also))
            def _():
                stage(t - lag)

        staged(1, average, is_hub)
        staged(2, update)
        staged(3, first_hop)
        staged(4, second_hop)
        staged(5, third_hop)
        staged(6, project)
        return 0

    lax.fori_loop(0, CHUNKS + 6, tick, 0)

    def drain(n, _):
        @pl.when(is_hub)
        def _():
            taken(sent.at[n, pl.ds(0, 3)], send.at[SA, n])
            taken(pool.at[n, pl.ds(8, slots)], send.at[SB, n])
            taken(means.at[n, pl.ds(0, 7)], send.at[SC, n])

        @pl.when(jnp.logical_not(is_hub))
        def _():
            taken(sent.at[n], send.at[SA, n])

        taken(weights.at[n, pl.ds(0, 15 * ROWS)], send.at[SW, n])
        outer_store(n).wait()
        moment_store(n).wait()
        kv_store(n).wait()
        return 0

    lax.fori_loop(0, CHUNKS, drain, 0)


def partner_table(matching):
    total_count = matching.shape[0]
    indices = jnp.arange(total_count, dtype=jnp.int32)
    matches = (matching[None, :] == indices[:, None]).astype(jnp.int32)
    position = jnp.sum(matches * indices[None, :], axis=1)
    mate_pos = position + 1 - 2 * (position % 2)
    picked = (indices[None, :] == mate_pos[:, None]).astype(jnp.int32)
    return jnp.sum(picked * matching[None, :], axis=1)


def pair_tables(matching):
    partner = partner_table(matching)
    order = jnp.arange(16, dtype=jnp.int32)
    replica_of = (order % 4) * 4 + (order // 8) * 2 + (order // 4) % 2
    mate = jnp.sum(jnp.where(replica_of[:, None] == order[None, :], partner[None, :], 0), axis=1)
    mate_item = (mate % 4) // 2 * 8 + (mate % 2) * 4 + mate // 4
    crosses = (mate_item // 8 != order // 8).astype(jnp.int32)
    ahead = (order[None, :] < order[:, None]) & (order[None, :] // 8 == order[:, None] // 8)
    rank = jnp.sum(jnp.where(ahead, crosses[None, :], 0), axis=1)
    mate_rank = jnp.sum(jnp.where(mate_item[:, None] == order[None, :], rank[None, :], 0), axis=1)
    whole = mate_item % 8 + 8 * crosses
    packed = jnp.where(crosses == 1, 8 + mate_rank, mate_item % 8)
    taken = (rank[None, :] == order[:, None] % 8) & (crosses[None, :] == 1) & (order[None, :] // 8 == order[:, None] // 8)
    listed = jnp.sum(jnp.where(taken, order[None, :] % 8, 0), axis=1)
    return jnp.concatenate([packed, listed, whole]).astype(jnp.int32), jnp.sum(crosses) // 2


def launch(slots, *operands):
    hbm = pl.BlockSpec(memory_space=pl.ANY)
    vmem = pl.BlockSpec(memory_space=pltpu.VMEM)
    smem = pl.BlockSpec(memory_space=pltpu.SMEM)
    return pl.pallas_call(
        functools.partial(kernel, slots),
        out_shape=(
            jax.ShapeDtypeStruct((ROWS, WIDTH), F32),
            jax.ShapeDtypeStruct((ROWS, WIDTH), BF16),
            jax.ShapeDtypeStruct((TOKENS, WIDTH), BF16),
        ),
        in_specs=[smem, hbm, hbm, hbm, hbm, vmem, vmem, vmem, vmem],
        out_specs=(hbm, hbm, hbm),
        scratch_shapes=[
            pltpu.VMEM((CHUNKS, ROWS, CW), F32),
            pltpu.VMEM((CHUNKS, ROWS, CW), BF16),
            pltpu.VMEM((CHUNKS, ROWS, CW), BF16),
            pltpu.VMEM((TOKENS, DEPTH), BF16),
            pltpu.VMEM((CHUNKS, 4, 2, GROUP, CW), BF16),
            pltpu.VMEM((CHUNKS, 8 + slots, 2, GROUP, CW), BF16),
            pltpu.VMEM((CHUNKS if slots < 8 else 1, slots, 2, GROUP, CW), BF16),
            pltpu.VMEM((CHUNKS, 8, 2, GROUP, CW), BF16),
            pltpu.VMEM((CHUNKS, 4, 2, GROUP, CW), BF16),
            pltpu.VMEM((CHUNKS, DEPTH, CW), BF16),
            pltpu.VMEM((CHUNKS, TOKENS, CW), BF16),
            pltpu.SemaphoreType.DMA((9, CHUNKS)),
            pltpu.SemaphoreType.DMA((4, CHUNKS)),
            pltpu.SemaphoreType.DMA((5, CHUNKS)),
            pltpu.SemaphoreType.DMA((1,)),
        ],
        compiler_params=pltpu.CompilerParams(
            collective_id=slots, has_side_effects=True, vmem_limit_bytes=62 * 2**20
        ),
    )(*operands)


def on_device(outer_weight, inner_weight, momentum, matching, tokens, norm_gain, kv_bias):
    table, count = pair_tables(matching)

    positions = (lax.axis_index("shard") * TOKENS + jnp.arange(TOKENS, dtype=jnp.int32)).astype(F32)
    exponents = jnp.arange(HEAD_DIM // 2, dtype=F32) * (2.0 / HEAD_DIM)
    angles = positions[:, None] * (rope_base ** (-exponents))[None, :]
    cosine, sine = jnp.cos(angles), jnp.sin(angles)
    cosine = jnp.concatenate([cosine, cosine], axis=1)
    sine = jnp.concatenate([-sine, sine], axis=1)

    new_outer, new_moment, kv = lax.switch(
        jnp.clip((count - 3) // 2, 0, 2),
        [functools.partial(launch, slots) for slots in (4, 6, 8)],
        table,
        outer_weight[0],
        inner_weight[0],
        momentum[0],
        tokens[0],
        norm_gain,
        kv_bias,
        cosine,
        sine,
    )
    return (new_outer[None], new_moment[None], kv[None])


def solution(mesh):
    in_specs = (
        P("replica", "shard", None),
        P("replica", "shard", None),
        P("replica", "shard", None),
        P(),
        P("replica", "shard", None),
        P("replica", None),
        P("replica", None),
    )
    out_specs = (
        P("replica", "shard", None),
        P("replica", "shard", None),
        P("replica", "shard", None),
    )
    return jax.shard_map(on_device, mesh=mesh, in_specs=in_specs, out_specs=out_specs, check_vma=False)
```

```python
import functools

import jax
import jax.numpy as jnp
import numpy as np
from jax import lax
from jax.experimental import pallas as pl
from jax.experimental.pallas import tpu as pltpu
from jax.sharding import PartitionSpec as P

MESH = pl.DeviceIdType.MESH
BF16 = jnp.bfloat16
F32 = jnp.float32

HEAD_DIM = 128
KEY_WIDTH = 1024
momentum_rate = 0.9
outer_rate = 0.7
gossip_rate = 0.5
norm_eps = 1e-06
rope_base = 1000000.0

ROWS = 320
WIDTH = 2048
TOKENS = 256
DEPTH = 5120
GROUP = ROWS // 4
HALF = ROWS // 2
CHUNKS = 16
CW = WIDTH // CHUNKS
AHEAD = 2
NORM_TICKS = 4
DIRECT = True
EDGE_AHEAD = 1
LAGS = (1, 2, 4, 5, 6, 7)

A, B, C, D, X1, X2, F1, F2, K, E = range(10)
SA, SB, SC, SW, SE = range(5)
LO, LI, OO, OM, OK = range(5)


def kernel(
    slots,
    match_ref,
    outer_hbm,
    inner_hbm,
    moment_hbm,
    token_hbm,
    gain_hbm,
    bias_hbm,
    turn_hbm,
    new_outer_hbm,
    new_moment_hbm,
    kv_hbm,
    outer,
    inner,
    moment,
    normed,
    sent,
    pool,
    crossing,
    means,
    pair,
    weights,
    kv,
    gain_ref,
    bias_ref,
    turn_ref,
    cos_ref,
    sin_ref,
    mate_ref,
    recv,
    send,
    local,
    single,
):
    r, s = lax.axis_index("replica"), lax.axis_index("shard")
    y, zl = r // 4, r % 4
    zh, x, core = s // 8, (s // 2) % 4, s % 2
    side = zl // 2
    hub_z = 1 + side
    is_hub = zl == hub_z
    far = 3 - zl
    edge = 3 * side

    def place(py, pz, ph, px, pc):
        return (py * 4 + pz, ph * 8 + px * 2 + pc)

    right, left = (x + 1) % 4, (x + 3) % 4
    to_core = place(y, zl, zh, x, 1 - core)
    to_right = place(y, zl, zh, right, core)
    to_left = place(y, zl, zh, left, core)
    to_far = place(y, zl, 1 - zh, x, core)

    def rows_of(ph, px, pc, start=0, size=ROWS):
        return pl.ds(pl.multiple_of((ph * 8 + px * 2 + pc) * ROWS + start, 16), size)

    def cols(n):
        return pl.ds(pl.multiple_of(n * CW, CW), CW)

    def remote(src, dst, ssem, rsem, device):
        pltpu.make_async_remote_copy(
            src_ref=src, dst_ref=dst, send_sem=ssem, recv_sem=rsem, device_id=device, device_id_type=MESH
        ).start()

    def taken(ref, sem):
        pltpu.make_async_copy(ref, ref, sem).wait()

    def loads(n):
        return (
            pltpu.make_async_copy(outer_hbm.at[:, cols(n)], outer.at[n], local.at[LO, n]),
            pltpu.make_async_copy(inner_hbm.at[:, cols(n)], inner.at[n], local.at[LI, n]),
        )

    def moment_load(n):
        return pltpu.make_async_copy(moment_hbm.at[:, cols(n)], moment.at[n], local.at[OM, n])

    token_load = pltpu.make_async_copy(token_hbm, normed, single.at[0])
    small_loads = (
        pltpu.make_async_copy(gain_hbm, gain_ref, single.at[1]),
        pltpu.make_async_copy(bias_hbm, bias_ref, single.at[2]),
        pltpu.make_async_copy(
            turn_hbm.at[pl.ds(pl.multiple_of(s * TOKENS, TOKENS), TOKENS)], turn_ref, single.at[3]
        ),
    )

    def start_loads(n, _):
        for copy in loads(n):
            copy.start()
        return 0

    lax.fori_loop(0, CHUNKS, start_loads, 0)
    token_load.start()
    for copy in small_loads:
        copy.start()

    def start_moment(n, _):
        moment_load(n).start()
        return 0

    lax.fori_loop(0, CHUNKS, start_moment, 0)

    barrier = pltpu.get_barrier_semaphore()

    def greet(device):
        pl.semaphore_signal(barrier, inc=1, device_id=device, device_id_type=MESH)

    for device in (to_core, to_right, to_left, to_far):
        greet(device)
    for step in range(1, 4):
        greet(place((y + step) % 4, zl, zh, x, core))

    @pl.when(is_hub)
    def _():
        for step in range(4):
            greet(place((y + step) % 4, edge, zh, x, core))
        greet(place(y, far, zh, x, core))
        pl.semaphore_wait(barrier, 12)

    @pl.when(jnp.logical_not(is_hub))
    def _():
        for step in range(4):
            greet(place((y + step) % 4, hub_z, zh, x, core))
        pl.semaphore_wait(barrier, 11)

    own_items = pl.ds((zl % 2) * 4, 4)
    edge_items = pl.ds((edge % 2) * 4, 4)
    item = (zl % 2) * 4 + y

    def send_rows(n):
        for copy in loads(n):
            copy.wait()

        def group(g, _):
            rows = pl.ds(pl.multiple_of(g * GROUP, 16), GROUP)
            own = outer[n, rows, :]
            sent[n, g, 0] = (own - inner[n, rows, :].astype(F32)).astype(BF16)
            sent[n, g, 1] = own.astype(BF16)
            return 0

        lax.fori_loop(0, 4, group, 0)
        for step in range(4):
            to_y = (y + step) % 4
            src, dst = sent.at[n, to_y], pool.at[n, item]
            if step:
                to_z = hub_z if DIRECT else zl
                remote(src, dst, send.at[SA, n], recv.at[A, n], place(to_y, to_z, zh, x, core))
            elif DIRECT:

                @pl.when(is_hub)
                def _():
                    pltpu.make_async_copy(src, dst, recv.at[A, n]).start()

                @pl.when(jnp.logical_not(is_hub))
                def _():
                    remote(src, dst, send.at[SA, n], recv.at[A, n], place(to_y, hub_z, zh, x, core))
            else:
                pltpu.make_async_copy(src, dst, recv.at[A, n]).start()

    def to_hub(n):
        taken(pool.at[n, own_items], recv.at[A, n])
        items = pool.at[n, own_items]
        remote(items, items, send.at[SE, n], recv.at[E, n], place(y, hub_z, zh, x, core))

    def swap_sides(n):
        if DIRECT:
            taken(pool.at[n, pl.ds(0, 8)], recv.at[A, n])
        else:
            taken(pool.at[n, own_items], recv.at[A, n])
            taken(pool.at[n, edge_items], recv.at[E, n])
        if slots < 8:

            def part(i, _):
                v = i // 5
                rows = pl.ds(pl.multiple_of((i % 5) * 16, 16), 16)
                held = [pool[n, j, v, rows, :] for j in range(8)]
                for k in range(slots):
                    which = mate_ref[8 + k]
                    value = held[0]
                    for j in range(1, 8):
                        value = jnp.where(which == j, held[j], value)
                    crossing[n, k, v, rows, :] = value
                return 0

            lax.fori_loop(0, 10, part, 0)
            src = crossing.at[n]
        else:
            src = pool.at[n, pl.ds(0, 8)]
        remote(src, pool.at[n, pl.ds(8, slots)], send.at[SB, n], recv.at[B, n], place(y, far, zh, x, core))

    def average(n):
        taken(pool.at[n, pl.ds(8, slots)], recv.at[B, n])
        mates = [mate_ref[k] for k in range(8)]

        def part(i, _):
            v = i // 5
            rows = pl.ds(pl.multiple_of((i % 5) * 16, 16), 16)
            held = [pool[n, j, v, rows, :] for j in range(8 + slots)]
            for k in range(8):
                value = held[0]
                for j in range(1, 8 + slots):
                    value = jnp.where(mates[k] == j, held[j], value)
                means[n, k, v, rows, :] = ((held[k].astype(F32) + value.astype(F32)) * 0.5).astype(BF16)
            return 0

        lax.fori_loop(0, 10, part, 0)
        for step in range(4):
            to_y = (y + step) % 4
            src, dst = means.at[n, (zl % 2) * 4 + to_y], pair.at[n, y]
            if step:
                remote(src, dst, send.at[SC, n], recv.at[C, n], place(to_y, zl, zh, x, core))
            else:
                pltpu.make_async_copy(src, dst, recv.at[C, n]).start()
            remote(
                means.at[n, (edge % 2) * 4 + to_y],
                dst,
                send.at[SC, n],
                recv.at[C, n],
                place(to_y, edge, zh, x, core),
            )

    def pass_on(n, rows, rsem, device):
        block = weights.at[n, rows]
        remote(block, block, send.at[SW, n], recv.at[rsem, n], device)

    def update(n):
        taken(pair.at[n], recv.at[C, n])
        moment_load(n).wait()

        def group(g, _):
            rows = pl.ds(pl.multiple_of(g * GROUP, 16), GROUP)
            own = outer[n, rows, :]
            delta = pair[n, g, 0].astype(F32)
            velocity = momentum_rate * moment[n, rows, :].astype(F32) + delta
            updated = (
                own
                - outer_rate * (delta + momentum_rate * velocity)
                - gossip_rate * (own - pair[n, g, 1].astype(F32))
            )
            outer[n, rows, :] = updated
            moment[n, rows, :] = velocity.astype(BF16)
            weights[n, pl.ds(pl.multiple_of(s * ROWS + g * GROUP, 16), GROUP), :] = updated.astype(BF16)
            return 0

        lax.fori_loop(0, 4, group, 0)
        own_rows = rows_of(zh, x, core)
        pass_on(n, own_rows, D, to_far)
        pass_on(n, own_rows, X1, to_right)
        pass_on(n, own_rows, X1, to_left)
        pass_on(n, own_rows, K, to_core)
        outer_store(n).start()
        moment_store(n).start()

    def outer_store(n):
        return pltpu.make_async_copy(outer.at[n], new_outer_hbm.at[:, cols(n)], local.at[OO, n])

    def moment_store(n):
        return pltpu.make_async_copy(moment.at[n], new_moment_hbm.at[:, cols(n)], local.at[OM, n])

    def kv_store(n):
        return pltpu.make_async_copy(kv.at[n], kv_hbm.at[:, cols(n)], local.at[OK, n])

    def forward(n, ph, rsem):
        pass_on(n, rows_of(ph, left, core, 0, HALF), rsem, to_right)
        pass_on(n, rows_of(ph, right, core, HALF, HALF), rsem, to_left)
        pass_on(n, rows_of(ph, left, core), K, to_core)
        pass_on(n, rows_of(ph, right, core), K, to_core)

    def first_hop(n):
        taken(weights.at[n, rows_of(1 - zh, x, core)], recv.at[D, n])
        far_rows = rows_of(1 - zh, x, core)
        pass_on(n, far_rows, X2, to_right)
        pass_on(n, far_rows, X2, to_left)
        pass_on(n, far_rows, K, to_core)
        taken(weights.at[n, pl.ds(0, 2 * ROWS)], recv.at[X1, n])
        forward(n, zh, F1)

    def second_hop(n):
        taken(weights.at[n, pl.ds(0, 2 * ROWS)], recv.at[X2, n])
        forward(n, 1 - zh, F2)
        taken(weights.at[n, pl.ds(0, ROWS)], recv.at[F1, n])
        pass_on(n, rows_of(zh, (x + 2) % 4, core), K, to_core)

    def third_hop(n):
        taken(weights.at[n, pl.ds(0, ROWS)], recv.at[F2, n])
        pass_on(n, rows_of(1 - zh, (x + 2) % 4, core), K, to_core)

    def norm_rows(t):
        @pl.when(t == 0)
        def _():
            token_load.wait()
            for copy in small_loads:
                copy.wait()
            turns = turn_ref[...]
            swapped = pltpu.roll(turns, HEAD_DIM // 2, 1)
            first = lax.broadcasted_iota(jnp.int32, turns.shape, 1) < HEAD_DIM // 2
            cos_ref[...] = jnp.where(first, turns, swapped)
            sin_ref[...] = jnp.where(first, -swapped, turns)

        per_tick = TOKENS // NORM_TICKS

        def part(i, _):
            rows = pl.ds(pl.multiple_of(t * per_tick + i * 16, 16), 16)
            values = normed[rows, :].astype(F32)
            mean_square = jnp.mean(values * values, axis=-1, keepdims=True)
            normed[rows, :] = (values * lax.rsqrt(mean_square + norm_eps) * gain_ref[...]).astype(BF16)
            return 0

        lax.fori_loop(0, per_tick // 16, part, 0)

    def project(n):
        taken(weights.at[n, pl.ds(0, DEPTH // 2)], recv.at[K, n])
        out = jnp.dot(normed[...], weights[n], preferred_element_type=F32) + bias_ref[:, cols(n)]

        @pl.when(n * CW < KEY_WIDTH)
        def _():
            for h in range(CW // HEAD_DIM):
                head = out[:, h * HEAD_DIM : (h + 1) * HEAD_DIM]
                turned = head * cos_ref[...] + pltpu.roll(head, HEAD_DIM // 2, 1) * sin_ref[...]
                kv[n, :, h * HEAD_DIM : (h + 1) * HEAD_DIM] = turned.astype(BF16)

        @pl.when(n * CW >= KEY_WIDTH)
        def _():
            kv[n] = out.astype(BF16)

        kv_store(n).start()

    def find_mates():
        found = [match_ref[p] for p in range(16)]

        def mate_of(on_side, k):
            replica = (k % 4) * 4 + on_side * 2 + k // 4
            mate = 0
            for p in range(16):
                mate = mate + jnp.where(found[p] == replica, found[p ^ 1], 0)
            crosses = jnp.where((mate // 2) % 2 != on_side, 1, 0)
            return (mate % 2) * 4 + mate // 4, crosses

        def ranks(crosses):
            return [sum(crosses[:k], 0) for k in range(8)]

        mates, crosses = zip(*[mate_of(side, k) for k in range(8)])
        if slots == 8:
            for k in range(8):
                mate_ref[k] = mates[k] + 8 * crosses[k]
            return
        rank = ranks(crosses)
        far_rank = ranks([mate_of(1 - side, k)[1] for k in range(8)])
        for k in range(8):
            place_far = 8
            for j in range(8):
                place_far = place_far + jnp.where(mates[k] == j, far_rank[j], 0)
            mate_ref[k] = jnp.where(crosses[k] == 1, place_far, mates[k])
        for slot in range(slots):
            which = 0
            for k in range(8):
                which = which + jnp.where(jnp.logical_and(crosses[k] == 1, rank[k] == slot), k, 0)
            mate_ref[8 + slot] = which

    def first_rows(n, _):
        send_rows(n)
        return 0

    lax.fori_loop(0, AHEAD, first_rows, 0)

    @pl.when(is_hub)
    def _():
        find_mates()

    if not DIRECT:

        @pl.when(jnp.logical_not(is_hub))
        def _():
            for n in range(EDGE_AHEAD):
                to_hub(n)

    def tick(t, _):
        @pl.when(t + AHEAD < CHUNKS)
        def _():
            send_rows(t + AHEAD)

        if not DIRECT:

            @pl.when(jnp.logical_and(jnp.logical_not(is_hub), t + EDGE_AHEAD < CHUNKS))
            def _():
                to_hub(t + EDGE_AHEAD)

        @pl.when(jnp.logical_and(is_hub, t < CHUNKS))
        def _():
            swap_sides(t)

        @pl.when(t < NORM_TICKS)
        def _():
            norm_rows(t)

        def staged(lag, stage, also=None):
            ready = jnp.logical_and(t >= lag, t < CHUNKS + lag)

            @pl.when(ready if also is None else jnp.logical_and(ready, also))
            def _():
                stage(t - lag)

        staged(LAGS[0], average, is_hub)
        staged(LAGS[1], update)
        staged(LAGS[2], first_hop)
        staged(LAGS[3], second_hop)
        staged(LAGS[4], third_hop)
        staged(LAGS[5], project)
        return 0

    lax.fori_loop(0, CHUNKS + LAGS[5], tick, 0)

    def drain(n, _):
        @pl.when(is_hub)
        def _():
            taken(sent.at[n, pl.ds(0, 3)], send.at[SA, n])
            taken(pool.at[n, pl.ds(8, slots)], send.at[SB, n])
            taken(means.at[n, pl.ds(0, 7)], send.at[SC, n])

        @pl.when(jnp.logical_not(is_hub))
        def _():
            if DIRECT:
                taken(sent.at[n], send.at[SA, n])
            else:
                taken(sent.at[n, pl.ds(0, 3)], send.at[SA, n])
                taken(pool.at[n, own_items], send.at[SE, n])

        taken(weights.at[n, pl.ds(0, 15 * ROWS)], send.at[SW, n])
        outer_store(n).wait()
        moment_store(n).wait()
        kv_store(n).wait()
        return 0

    lax.fori_loop(0, CHUNKS, drain, 0)


def turn_table(tokens):
    exponents = np.arange(HEAD_DIM // 2, dtype=np.float32) * np.float32(2.0 / HEAD_DIM)
    inverse = (rope_base ** (-exponents.astype(np.float64))).astype(np.float32)
    angles = np.arange(tokens, dtype=np.float32)[:, None] * inverse[None, :]
    angles = angles.astype(np.float64)
    return np.concatenate([np.cos(angles), np.sin(angles)], axis=1).astype(np.float32)


def launch(slots, *operands):
    hbm = pl.BlockSpec(memory_space=pl.ANY)
    smem = pl.BlockSpec(memory_space=pltpu.SMEM)
    return pl.pallas_call(
        functools.partial(kernel, slots),
        out_shape=(
            jax.ShapeDtypeStruct((ROWS, WIDTH), F32),
            jax.ShapeDtypeStruct((ROWS, WIDTH), BF16),
            jax.ShapeDtypeStruct((TOKENS, WIDTH), BF16),
        ),
        in_specs=[smem] + [hbm] * 7,
        out_specs=(hbm, hbm, hbm),
        scratch_shapes=[
            pltpu.VMEM((CHUNKS, ROWS, CW), F32),
            pltpu.VMEM((CHUNKS, ROWS, CW), BF16),
            pltpu.VMEM((CHUNKS, ROWS, CW), BF16),
            pltpu.VMEM((TOKENS, DEPTH), BF16),
            pltpu.VMEM((CHUNKS, 4, 2, GROUP, CW), BF16),
            pltpu.VMEM((CHUNKS, 8 + slots, 2, GROUP, CW), BF16),
            pltpu.VMEM((CHUNKS if slots < 8 else 1, slots, 2, GROUP, CW), BF16),
            pltpu.VMEM((CHUNKS, 8, 2, GROUP, CW), BF16),
            pltpu.VMEM((CHUNKS, 4, 2, GROUP, CW), BF16),
            pltpu.VMEM((CHUNKS, DEPTH, CW), BF16),
            pltpu.VMEM((CHUNKS, TOKENS, CW), BF16),
            pltpu.VMEM((1, DEPTH), F32),
            pltpu.VMEM((1, WIDTH), F32),
            pltpu.VMEM((TOKENS, HEAD_DIM), F32),
            pltpu.VMEM((TOKENS, HEAD_DIM), F32),
            pltpu.VMEM((TOKENS, HEAD_DIM), F32),
            pltpu.SMEM((16,), jnp.int32),
            pltpu.SemaphoreType.DMA((10, CHUNKS)),
            pltpu.SemaphoreType.DMA((5, CHUNKS)),
            pltpu.SemaphoreType.DMA((5, CHUNKS)),
            pltpu.SemaphoreType.DMA((4,)),
        ],
        compiler_params=pltpu.CompilerParams(
            collective_id=slots, has_side_effects=True, vmem_limit_bytes=62 * 2**20
        ),
    )(*operands)


def on_device(outer_weight, inner_weight, momentum, matching, tokens, norm_gain, kv_bias):
    sides = (matching // 2) % 2
    count = jnp.sum(sides.reshape(8, 2)[:, 0] != sides.reshape(8, 2)[:, 1])
    turns = jnp.asarray(turn_table(TOKENS * lax.axis_size("shard")))

    new_outer, new_moment, kv = lax.switch(
        jnp.clip((count - 3) // 2, 0, 2),
        [functools.partial(launch, slots) for slots in (4, 6, 8)],
        matching,
        outer_weight[0],
        inner_weight[0],
        momentum[0],
        tokens[0],
        norm_gain,
        kv_bias,
        turns,
    )
    return (new_outer[None], new_moment[None], kv[None])


def solution(mesh):
    in_specs = (
        P("replica", "shard", None),
        P("replica", "shard", None),
        P("replica", "shard", None),
        P(),
        P("replica", "shard", None),
        P("replica", None),
        P("replica", None),
    )
    out_specs = (
        P("replica", "shard", None),
        P("replica", "shard", None),
        P("replica", "shard", None),
    )
    return jax.shard_map(on_device, mesh=mesh, in_specs=in_specs, out_specs=out_specs, check_vma=False)
```

```python
import functools

import jax
import jax.numpy as jnp
import numpy as np
from jax import lax
from jax.experimental import pallas as pl
from jax.experimental.pallas import tpu as pltpu
from jax.sharding import PartitionSpec as P

MESH = pl.DeviceIdType.MESH
BF16 = jnp.bfloat16
F32 = jnp.float32

HEAD_DIM = 128
KEY_WIDTH = 1024
momentum_rate = 0.9
outer_rate = 0.7
gossip_rate = 0.5
norm_eps = 1e-06
rope_base = 1000000.0

ROWS = 320
WIDTH = 2048
TOKENS = 256
DEPTH = 5120
GROUP = ROWS // 4
HALF = ROWS // 2
CHUNKS = 16
CW = WIDTH // CHUNKS
AHEAD = 2
NORM_TICKS = 4
DIRECT = True
EDGE_AHEAD = 1
LAGS = (1, 2, 4, 5, 6, 7)

A, B, C, D, X1, X2, F1, F2, K, E = range(10)
SA, SB, SC, SW, SE = range(5)
LO, LI, OO, OM, OK = range(5)


def kernel(
    slots,
    match_ref,
    outer_hbm,
    inner_hbm,
    moment_hbm,
    token_hbm,
    gain_hbm,
    bias_hbm,
    turn_hbm,
    new_outer_hbm,
    new_moment_hbm,
    kv_hbm,
    outer,
    inner,
    moment,
    normed,
    sent,
    pool,
    crossing,
    means,
    pair,
    weights,
    kv,
    gain_ref,
    bias_ref,
    turn_ref,
    cos_ref,
    sin_ref,
    mate_ref,
    recv,
    send,
    local,
    single,
):
    r, s = lax.axis_index("replica"), lax.axis_index("shard")
    y, zl = r // 4, r % 4
    zh, x, core = s // 8, (s // 2) % 4, s % 2
    side = zl // 2
    hub_z = 1 + side
    is_hub = zl == hub_z
    far = 3 - zl
    edge = 3 * side

    def place(py, pz, ph, px, pc):
        return (py * 4 + pz, ph * 8 + px * 2 + pc)

    right, left = (x + 1) % 4, (x + 3) % 4
    to_core = place(y, zl, zh, x, 1 - core)
    to_right = place(y, zl, zh, right, core)
    to_left = place(y, zl, zh, left, core)
    to_far = place(y, zl, 1 - zh, x, core)

    def rows_of(ph, px, pc, start=0, size=ROWS):
        return pl.ds(pl.multiple_of((ph * 8 + px * 2 + pc) * ROWS + start, 16), size)

    def cols(n):
        return pl.ds(pl.multiple_of(n * CW, CW), CW)

    def remote(src, dst, ssem, rsem, device):
        pltpu.make_async_remote_copy(
            src_ref=src, dst_ref=dst, send_sem=ssem, recv_sem=rsem, device_id=device, device_id_type=MESH
        ).start()

    def taken(ref, sem):
        pltpu.make_async_copy(ref, ref, sem).wait()

    def loads(n):
        return (
            pltpu.make_async_copy(outer_hbm.at[:, cols(n)], outer.at[n], local.at[LO, n]),
            pltpu.make_async_copy(inner_hbm.at[:, cols(n)], inner.at[n], local.at[LI, n]),
        )

    def moment_load(n):
        return pltpu.make_async_copy(moment_hbm.at[:, cols(n)], moment.at[n], local.at[OM, n])

    token_load = pltpu.make_async_copy(token_hbm, normed, single.at[0])
    small_loads = (
        pltpu.make_async_copy(gain_hbm, gain_ref, single.at[1]),
        pltpu.make_async_copy(bias_hbm, bias_ref, single.at[2]),
        pltpu.make_async_copy(
            turn_hbm.at[pl.ds(pl.multiple_of(s * TOKENS, TOKENS), TOKENS)], turn_ref, single.at[3]
        ),
    )

    def start_loads(n, _):
        for copy in loads(n):
            copy.start()
        return 0

    lax.fori_loop(0, CHUNKS, start_loads, 0)
    token_load.start()
    for copy in small_loads:
        copy.start()

    def start_moment(n, _):
        moment_load(n).start()
        return 0

    lax.fori_loop(0, CHUNKS, start_moment, 0)

    barrier = pltpu.get_barrier_semaphore()

    def greet(device):
        pl.semaphore_signal(barrier, inc=1, device_id=device, device_id_type=MESH)

    for device in (to_core, to_right, to_left, to_far):
        greet(device)
    for step in range(1, 4):
        greet(place((y + step) % 4, zl, zh, x, core))

    @pl.when(is_hub)
    def _():
        for step in range(4):
            greet(place((y + step) % 4, edge, zh, x, core))
        greet(place(y, far, zh, x, core))
        pl.semaphore_wait(barrier, 12)

    @pl.when(jnp.logical_not(is_hub))
    def _():
        for step in range(4):
            greet(place((y + step) % 4, hub_z, zh, x, core))
        pl.semaphore_wait(barrier, 11)

    own_items = pl.ds((zl % 2) * 4, 4)
    edge_items = pl.ds((edge % 2) * 4, 4)
    item = (zl % 2) * 4 + y

    def send_rows(n):
        for copy in loads(n):
            copy.wait()

        def group(g, _):
            rows = pl.ds(pl.multiple_of(g * GROUP, 16), GROUP)
            own = outer[n, rows, :]
            sent[n, g, 0] = (own - inner[n, rows, :].astype(F32)).astype(BF16)
            sent[n, g, 1] = own.astype(BF16)
            return 0

        lax.fori_loop(0, 4, group, 0)
        for step in range(4):
            to_y = (y + step) % 4
            src, dst = sent.at[n, to_y], pool.at[n, item]
            if step:
                to_z = hub_z if DIRECT else zl
                remote(src, dst, send.at[SA, n], recv.at[A, n], place(to_y, to_z, zh, x, core))
            elif DIRECT:

                @pl.when(is_hub)
                def _():
                    pltpu.make_async_copy(src, dst, recv.at[A, n]).start()

                @pl.when(jnp.logical_not(is_hub))
                def _():
                    remote(src, dst, send.at[SA, n], recv.at[A, n], place(to_y, hub_z, zh, x, core))
            else:
                pltpu.make_async_copy(src, dst, recv.at[A, n]).start()

    def to_hub(n):
        taken(pool.at[n, own_items], recv.at[A, n])
        items = pool.at[n, own_items]
        remote(items, items, send.at[SE, n], recv.at[E, n], place(y, hub_z, zh, x, core))

    def swap_sides(n):
        if DIRECT:
            taken(pool.at[n, pl.ds(0, 8)], recv.at[A, n])
        else:
            taken(pool.at[n, own_items], recv.at[A, n])
            taken(pool.at[n, edge_items], recv.at[E, n])
        if slots < 8:

            def part(i, _):
                v = i // 5
                rows = pl.ds(pl.multiple_of((i % 5) * 16, 16), 16)
                held = [pool[n, j, v, rows, :] for j in range(8)]
                for k in range(slots):
                    which = mate_ref[8 + k]
                    value = held[0]
                    for j in range(1, 8):
                        value = jnp.where(which == j, held[j], value)
                    crossing[n, k, v, rows, :] = value
                return 0

            lax.fori_loop(0, 10, part, 0)
            src = crossing.at[n]
        else:
            src = pool.at[n, pl.ds(0, 8)]
        remote(src, pool.at[n, pl.ds(8, slots)], send.at[SB, n], recv.at[B, n], place(y, far, zh, x, core))

    def average(n):
        taken(pool.at[n, pl.ds(8, slots)], recv.at[B, n])
        mates = [mate_ref[k] for k in range(8)]

        def part(i, _):
            v = i // 5
            rows = pl.ds(pl.multiple_of((i % 5) * 16, 16), 16)
            held = [pool[n, j, v, rows, :] for j in range(8 + slots)]
            for k in range(8):
                value = held[0]
                for j in range(1, 8 + slots):
                    value = jnp.where(mates[k] == j, held[j], value)
                means[n, k, v, rows, :] = ((held[k].astype(F32) + value.astype(F32)) * 0.5).astype(BF16)
            return 0

        lax.fori_loop(0, 10, part, 0)
        for step in range(4):
            to_y = (y + step) % 4
            src, dst = means.at[n, (zl % 2) * 4 + to_y], pair.at[n, y]
            if step:
                remote(src, dst, send.at[SC, n], recv.at[C, n], place(to_y, zl, zh, x, core))
            else:
                pltpu.make_async_copy(src, dst, recv.at[C, n]).start()
            remote(
                means.at[n, (edge % 2) * 4 + to_y],
                dst,
                send.at[SC, n],
                recv.at[C, n],
                place(to_y, edge, zh, x, core),
            )

    def pass_on(n, rows, rsem, device):
        block = weights.at[n, rows]
        remote(block, block, send.at[SW, n], recv.at[rsem, n], device)

    def update(n):
        taken(pair.at[n], recv.at[C, n])
        moment_load(n).wait()

        def group(g, _):
            rows = pl.ds(pl.multiple_of(g * GROUP, 16), GROUP)
            own = outer[n, rows, :]
            delta = pair[n, g, 0].astype(F32)
            velocity = momentum_rate * moment[n, rows, :].astype(F32) + delta
            updated = (
                own
                - outer_rate * (delta + momentum_rate * velocity)
                - gossip_rate * (own - pair[n, g, 1].astype(F32))
            )
            outer[n, rows, :] = updated
            moment[n, rows, :] = velocity.astype(BF16)
            weights[n, pl.ds(pl.multiple_of(s * ROWS + g * GROUP, 16), GROUP), :] = updated.astype(BF16)
            return 0

        lax.fori_loop(0, 4, group, 0)
        own_rows = rows_of(zh, x, core)
        pass_on(n, own_rows, D, to_far)
        pass_on(n, own_rows, X1, to_right)
        pass_on(n, own_rows, X1, to_left)
        pass_on(n, own_rows, K, to_core)
        outer_store(n).start()
        moment_store(n).start()

    def outer_store(n):
        return pltpu.make_async_copy(outer.at[n], new_outer_hbm.at[:, cols(n)], local.at[OO, n])

    def moment_store(n):
        return pltpu.make_async_copy(moment.at[n], new_moment_hbm.at[:, cols(n)], local.at[OM, n])

    def kv_store(n):
        return pltpu.make_async_copy(kv.at[n], kv_hbm.at[:, cols(n)], local.at[OK, n])

    def forward(n, ph, rsem):
        pass_on(n, rows_of(ph, left, core, 0, HALF), rsem, to_right)
        pass_on(n, rows_of(ph, right, core, HALF, HALF), rsem, to_left)
        pass_on(n, rows_of(ph, left, core), K, to_core)
        pass_on(n, rows_of(ph, right, core), K, to_core)

    def first_hop(n):
        taken(weights.at[n, rows_of(1 - zh, x, core)], recv.at[D, n])
        far_rows = rows_of(1 - zh, x, core)
        pass_on(n, far_rows, X2, to_right)
        pass_on(n, far_rows, X2, to_left)
        pass_on(n, far_rows, K, to_core)
        taken(weights.at[n, pl.ds(0, 2 * ROWS)], recv.at[X1, n])
        forward(n, zh, F1)

    def second_hop(n):
        taken(weights.at[n, pl.ds(0, 2 * ROWS)], recv.at[X2, n])
        forward(n, 1 - zh, F2)
        taken(weights.at[n, pl.ds(0, ROWS)], recv.at[F1, n])
        pass_on(n, rows_of(zh, (x + 2) % 4, core), K, to_core)

    def third_hop(n):
        taken(weights.at[n, pl.ds(0, ROWS)], recv.at[F2, n])
        pass_on(n, rows_of(1 - zh, (x + 2) % 4, core), K, to_core)

    def norm_rows(t):
        @pl.when(t == 0)
        def _():
            token_load.wait()
            for copy in small_loads:
                copy.wait()
            turns = turn_ref[...]
            swapped = pltpu.roll(turns, HEAD_DIM // 2, 1)
            first = lax.broadcasted_iota(jnp.int32, turns.shape, 1) < HEAD_DIM // 2
            cos_ref[...] = jnp.where(first, turns, swapped)
            sin_ref[...] = jnp.where(first, -swapped, turns)

        per_tick = TOKENS // NORM_TICKS

        def part(i, _):
            rows = pl.ds(pl.multiple_of(t * per_tick + i * 16, 16), 16)
            values = normed[rows, :].astype(F32)
            mean_square = jnp.mean(values * values, axis=-1, keepdims=True)
            normed[rows, :] = (values * lax.rsqrt(mean_square + norm_eps) * gain_ref[...]).astype(BF16)
            return 0

        lax.fori_loop(0, per_tick // 16, part, 0)

    def project(n):
        taken(weights.at[n, pl.ds(0, DEPTH // 2)], recv.at[K, n])
        out = jnp.dot(normed[...], weights[n], preferred_element_type=F32) + bias_ref[:, cols(n)]

        @pl.when(n * CW < KEY_WIDTH)
        def _():
            for h in range(CW // HEAD_DIM):
                head = out[:, h * HEAD_DIM : (h + 1) * HEAD_DIM]
                turned = head * cos_ref[...] + pltpu.roll(head, HEAD_DIM // 2, 1) * sin_ref[...]
                kv[n, :, h * HEAD_DIM : (h + 1) * HEAD_DIM] = turned.astype(BF16)

        @pl.when(n * CW >= KEY_WIDTH)
        def _():
            kv[n] = out.astype(BF16)

        kv_store(n).start()

    def find_mates():
        found = [match_ref[p] for p in range(16)]

        def mate_of(on_side, k):
            replica = (k % 4) * 4 + on_side * 2 + k // 4
            mate = 0
            for p in range(16):
                mate = mate + jnp.where(found[p] == replica, found[p ^ 1], 0)
            crosses = jnp.where((mate // 2) % 2 != on_side, 1, 0)
            return (mate % 2) * 4 + mate // 4, crosses

        def ranks(crosses):
            return [sum(crosses[:k], 0) for k in range(8)]

        mates, crosses = zip(*[mate_of(side, k) for k in range(8)])
        if slots == 8:
            for k in range(8):
                mate_ref[k] = mates[k] + 8 * crosses[k]
            return
        rank = ranks(crosses)
        far_rank = ranks([mate_of(1 - side, k)[1] for k in range(8)])
        for k in range(8):
            place_far = 8
            for j in range(8):
                place_far = place_far + jnp.where(mates[k] == j, far_rank[j], 0)
            mate_ref[k] = jnp.where(crosses[k] == 1, place_far, mates[k])
        for slot in range(slots):
            which = 0
            for k in range(8):
                which = which + jnp.where(jnp.logical_and(crosses[k] == 1, rank[k] == slot), k, 0)
            mate_ref[8 + slot] = which

    def first_rows(n, _):
        send_rows(n)
        return 0

    lax.fori_loop(0, AHEAD, first_rows, 0)

    @pl.when(is_hub)
    def _():
        find_mates()

    if not DIRECT:

        @pl.when(jnp.logical_not(is_hub))
        def _():
            for n in range(EDGE_AHEAD):
                to_hub(n)

    def tick(t, _):
        @pl.when(t + AHEAD < CHUNKS)
        def _():
            send_rows(t + AHEAD)

        if not DIRECT:

            @pl.when(jnp.logical_and(jnp.logical_not(is_hub), t + EDGE_AHEAD < CHUNKS))
            def _():
                to_hub(t + EDGE_AHEAD)

        @pl.when(jnp.logical_and(is_hub, t < CHUNKS))
        def _():
            swap_sides(t)

        @pl.when(t < NORM_TICKS)
        def _():
            norm_rows(t)

        def staged(lag, stage, also=None):
            ready = jnp.logical_and(t >= lag, t < CHUNKS + lag)

            @pl.when(ready if also is None else jnp.logical_and(ready, also))
            def _():
                stage(t - lag)

        staged(LAGS[0], average, is_hub)
        staged(LAGS[1], update)
        staged(LAGS[2], first_hop)
        staged(LAGS[3], second_hop)
        staged(LAGS[4], third_hop)
        staged(LAGS[5], project)
        return 0

    lax.fori_loop(0, CHUNKS + LAGS[5], tick, 0)

    def drain(n, _):
        @pl.when(is_hub)
        def _():
            taken(sent.at[n, pl.ds(0, 3)], send.at[SA, n])
            taken(pool.at[n, pl.ds(8, slots)], send.at[SB, n])
            taken(means.at[n, pl.ds(0, 7)], send.at[SC, n])

        @pl.when(jnp.logical_not(is_hub))
        def _():
            if DIRECT:
                taken(sent.at[n], send.at[SA, n])
            else:
                taken(sent.at[n, pl.ds(0, 3)], send.at[SA, n])
                taken(pool.at[n, own_items], send.at[SE, n])

        taken(weights.at[n, pl.ds(0, 15 * ROWS)], send.at[SW, n])
        outer_store(n).wait()
        moment_store(n).wait()
        kv_store(n).wait()
        return 0

    lax.fori_loop(0, CHUNKS, drain, 0)


def turn_table(tokens):
    exponents = np.arange(HEAD_DIM // 2, dtype=np.float32) * np.float32(2.0 / HEAD_DIM)
    inverse = (rope_base ** (-exponents.astype(np.float64))).astype(np.float32)
    angles = np.arange(tokens, dtype=np.float32)[:, None] * inverse[None, :]
    angles = angles.astype(np.float64)
    return np.concatenate([np.cos(angles), np.sin(angles)], axis=1).astype(np.float32)


def launch(slots, *operands):
    hbm = pl.BlockSpec(memory_space=pl.ANY)
    smem = pl.BlockSpec(memory_space=pltpu.SMEM)
    return pl.pallas_call(
        functools.partial(kernel, slots),
        out_shape=(
            jax.ShapeDtypeStruct((ROWS, WIDTH), F32),
            jax.ShapeDtypeStruct((ROWS, WIDTH), BF16),
            jax.ShapeDtypeStruct((TOKENS, WIDTH), BF16),
        ),
        in_specs=[smem] + [hbm] * 7,
        out_specs=(hbm, hbm, hbm),
        scratch_shapes=[
            pltpu.VMEM((CHUNKS, ROWS, CW), F32),
            pltpu.VMEM((CHUNKS, ROWS, CW), BF16),
            pltpu.VMEM((CHUNKS, ROWS, CW), BF16),
            pltpu.VMEM((TOKENS, DEPTH), BF16),
            pltpu.VMEM((CHUNKS, 4, 2, GROUP, CW), BF16),
            pltpu.VMEM((CHUNKS, 8 + slots, 2, GROUP, CW), BF16),
            pltpu.VMEM((CHUNKS if slots < 8 else 1, slots, 2, GROUP, CW), BF16),
            pltpu.VMEM((CHUNKS, 8, 2, GROUP, CW), BF16),
            pltpu.VMEM((CHUNKS, 4, 2, GROUP, CW), BF16),
            pltpu.VMEM((CHUNKS, DEPTH, CW), BF16),
            pltpu.VMEM((CHUNKS, TOKENS, CW), BF16),
            pltpu.VMEM((1, DEPTH), F32),
            pltpu.VMEM((1, WIDTH), F32),
            pltpu.VMEM((TOKENS, HEAD_DIM), F32),
            pltpu.VMEM((TOKENS, HEAD_DIM), F32),
            pltpu.VMEM((TOKENS, HEAD_DIM), F32),
            pltpu.SMEM((16,), jnp.int32),
            pltpu.SemaphoreType.DMA((10, CHUNKS)),
            pltpu.SemaphoreType.DMA((5, CHUNKS)),
            pltpu.SemaphoreType.DMA((5, CHUNKS)),
            pltpu.SemaphoreType.DMA((4,)),
        ],
        compiler_params=pltpu.CompilerParams(
            collective_id=slots, has_side_effects=True, vmem_limit_bytes=62 * 2**20
        ),
    )(*operands)


def copy_kernel(*refs):
    sems = refs[-1]
    loads, stores = [], []
    for src, dst, held, parts in zip(refs[:3], refs[3:6], refs[6:9], (8, 4, 4)):
        size = src.shape[0] // parts
        for i in range(parts):
            rows, j = pl.ds(i * size, size), len(loads)
            loads.append(pltpu.make_async_copy(src.at[rows], held.at[rows], sems.at[0, j]))
            stores.append(pltpu.make_async_copy(held.at[rows], dst.at[rows], sems.at[1, j]))
    for load in loads:
        load.start()
    for load, store in zip(loads, stores):
        load.wait()
        store.start()
    for store in stores:
        store.wait()


def copied(*arrays):
    hbm = pl.BlockSpec(memory_space=pl.ANY)
    return pl.pallas_call(
        copy_kernel,
        out_shape=tuple(jax.ShapeDtypeStruct(a.shape, a.dtype) for a in arrays),
        in_specs=[hbm] * 3,
        out_specs=(hbm,) * 3,
        scratch_shapes=[pltpu.VMEM(a.shape, a.dtype) for a in arrays] + [pltpu.SemaphoreType.DMA((2, 16))],
        compiler_params=pltpu.CompilerParams(vmem_limit_bytes=16 * 2**20),
    )(*arrays)


def on_device(outer_weight, inner_weight, momentum, matching, tokens, norm_gain, kv_bias):
    order = jnp.arange(16, dtype=jnp.int32)
    paired = (order[None, :] == order[:, None] + 1) & (order[:, None] % 2 == 0)
    count = jnp.sum(jnp.where(paired, ((matching[None, :] ^ matching[:, None]) >> 1) & 1, 0))
    turns = jnp.asarray(turn_table(TOKENS * lax.axis_size("shard")))

    new_outer, new_moment, kv = lax.switch(
        jnp.clip((count - 3) // 2, 0, 2),
        [functools.partial(launch, slots) for slots in (4, 6, 8)],
        matching,
        outer_weight[0],
        inner_weight[0],
        momentum[0],
        tokens[0],
        norm_gain,
        kv_bias,
        turns,
    )
    new_outer, new_moment, kv = copied(new_outer, new_moment, kv)
    return (new_outer[None], new_moment[None], kv[None])


def solution(mesh):
    in_specs = (
        P("replica", "shard", None),
        P("replica", "shard", None),
        P("replica", "shard", None),
        P(),
        P("replica", "shard", None),
        P("replica", None),
        P("replica", None),
    )
    out_specs = (
        P("replica", "shard", None),
        P("replica", "shard", None),
        P("replica", "shard", None),
    )
    return jax.shard_map(on_device, mesh=mesh, in_specs=in_specs, out_specs=out_specs, check_vma=False)
```

```python
import functools

import jax
import jax.numpy as jnp
import numpy as np
from jax import lax
from jax.experimental import pallas as pl
from jax.experimental.pallas import tpu as pltpu
from jax.sharding import PartitionSpec as P

MESH = pl.DeviceIdType.MESH
BF16 = jnp.bfloat16
F32 = jnp.float32

HEAD_DIM = 128
KEY_WIDTH = 1024
momentum_rate = 0.9
outer_rate = 0.7
gossip_rate = 0.5
norm_eps = 1e-06
rope_base = 1000000.0

ROWS = 320
WIDTH = 2048
TOKENS = 256
DEPTH = 5120
GROUP = ROWS // 4
HALF = ROWS // 2
CHUNKS = 16
CW = WIDTH // CHUNKS
AHEAD = 2
NORM_TICKS = 4
DIRECT = True
EDGE_AHEAD = 1
LAGS = (1, 2, 4, 5, 6, 7)

A, B, C, D, X1, X2, F1, F2, K, E = range(10)
SA, SB, SC, SW, SE = range(5)
LO, LI, OO, OM, OK = range(5)


def kernel(
    slots,
    match_ref,
    outer_hbm,
    inner_hbm,
    moment_hbm,
    token_hbm,
    gain_hbm,
    bias_hbm,
    turn_hbm,
    new_outer_hbm,
    new_moment_hbm,
    kv_hbm,
    outer,
    inner,
    moment,
    normed,
    sent,
    pool,
    crossing,
    means,
    pair,
    weights,
    kv,
    gain_ref,
    bias_ref,
    turn_ref,
    cos_ref,
    sin_ref,
    mate_ref,
    recv,
    send,
    local,
    single,
):
    r, s = lax.axis_index("replica"), lax.axis_index("shard")
    y, zl = r // 4, r % 4
    zh, x, core = s // 8, (s // 2) % 4, s % 2
    side = zl // 2
    hub_z = 1 + side
    is_hub = zl == hub_z
    far = 3 - zl
    edge = 3 * side

    def place(py, pz, ph, px, pc):
        return (py * 4 + pz, ph * 8 + px * 2 + pc)

    right, left = (x + 1) % 4, (x + 3) % 4
    to_core = place(y, zl, zh, x, 1 - core)
    to_right = place(y, zl, zh, right, core)
    to_left = place(y, zl, zh, left, core)
    to_far = place(y, zl, 1 - zh, x, core)

    def rows_of(ph, px, pc, start=0, size=ROWS):
        return pl.ds(pl.multiple_of((ph * 8 + px * 2 + pc) * ROWS + start, 16), size)

    def cols(n):
        return pl.ds(pl.multiple_of(n * CW, CW), CW)

    def remote(src, dst, ssem, rsem, device):
        pltpu.make_async_remote_copy(
            src_ref=src, dst_ref=dst, send_sem=ssem, recv_sem=rsem, device_id=device, device_id_type=MESH
        ).start()

    def taken(ref, sem):
        pltpu.make_async_copy(ref, ref, sem).wait()

    def loads(n):
        return (
            pltpu.make_async_copy(outer_hbm.at[:, cols(n)], outer.at[n], local.at[LO, n]),
            pltpu.make_async_copy(inner_hbm.at[:, cols(n)], inner.at[n], local.at[LI, n]),
        )

    def moment_load(n):
        return pltpu.make_async_copy(moment_hbm.at[:, cols(n)], moment.at[n], local.at[OM, n])

    token_load = pltpu.make_async_copy(token_hbm, normed, single.at[0])
    small_loads = (
        pltpu.make_async_copy(gain_hbm, gain_ref, single.at[1]),
        pltpu.make_async_copy(bias_hbm, bias_ref, single.at[2]),
        pltpu.make_async_copy(
            turn_hbm.at[pl.ds(pl.multiple_of(s * TOKENS, TOKENS), TOKENS)], turn_ref, single.at[3]
        ),
    )

    def start_loads(n, _):
        for copy in loads(n):
            copy.start()
        return 0

    lax.fori_loop(0, CHUNKS, start_loads, 0)
    token_load.start()
    for copy in small_loads:
        copy.start()

    def start_moment(n, _):
        moment_load(n).start()
        return 0

    lax.fori_loop(0, CHUNKS, start_moment, 0)

    barrier = pltpu.get_barrier_semaphore()

    def greet(device):
        pl.semaphore_signal(barrier, inc=1, device_id=device, device_id_type=MESH)

    for device in (to_core, to_right, to_left, to_far):
        greet(device)
    for step in range(1, 4):
        greet(place((y + step) % 4, zl, zh, x, core))

    @pl.when(is_hub)
    def _():
        for step in range(4):
            greet(place((y + step) % 4, edge, zh, x, core))
        greet(place(y, far, zh, x, core))
        pl.semaphore_wait(barrier, 12)

    @pl.when(jnp.logical_not(is_hub))
    def _():
        for step in range(4):
            greet(place((y + step) % 4, hub_z, zh, x, core))
        pl.semaphore_wait(barrier, 11)

    own_items = pl.ds((zl % 2) * 4, 4)
    edge_items = pl.ds((edge % 2) * 4, 4)
    item = (zl % 2) * 4 + y

    def send_rows(n):
        for copy in loads(n):
            copy.wait()

        def group(g, _):
            rows = pl.ds(pl.multiple_of(g * GROUP, 16), GROUP)
            own = outer[n, rows, :]
            sent[n, g, 0] = (own - inner[n, rows, :].astype(F32)).astype(BF16)
            sent[n, g, 1] = own.astype(BF16)
            return 0

        lax.fori_loop(0, 4, group, 0)
        for step in range(4):
            to_y = (y + step) % 4
            src, dst = sent.at[n, to_y], pool.at[n, item]
            if step:
                to_z = hub_z if DIRECT else zl
                remote(src, dst, send.at[SA, n], recv.at[A, n], place(to_y, to_z, zh, x, core))
            elif DIRECT:

                @pl.when(is_hub)
                def _():
                    pltpu.make_async_copy(src, dst, recv.at[A, n]).start()

                @pl.when(jnp.logical_not(is_hub))
                def _():
                    remote(src, dst, send.at[SA, n], recv.at[A, n], place(to_y, hub_z, zh, x, core))
            else:
                pltpu.make_async_copy(src, dst, recv.at[A, n]).start()

    def to_hub(n):
        taken(pool.at[n, own_items], recv.at[A, n])
        items = pool.at[n, own_items]
        remote(items, items, send.at[SE, n], recv.at[E, n], place(y, hub_z, zh, x, core))

    def swap_sides(n):
        if DIRECT:
            taken(pool.at[n, pl.ds(0, 8)], recv.at[A, n])
        else:
            taken(pool.at[n, own_items], recv.at[A, n])
            taken(pool.at[n, edge_items], recv.at[E, n])
        if slots < 8:

            def part(i, _):
                v = i // 5
                rows = pl.ds(pl.multiple_of((i % 5) * 16, 16), 16)
                held = [pool[n, j, v, rows, :] for j in range(8)]
                for k in range(slots):
                    which = mate_ref[8 + k]
                    value = held[0]
                    for j in range(1, 8):
                        value = jnp.where(which == j, held[j], value)
                    crossing[n, k, v, rows, :] = value
                return 0

            lax.fori_loop(0, 10, part, 0)
            src = crossing.at[n]
        else:
            src = pool.at[n, pl.ds(0, 8)]
        remote(src, pool.at[n, pl.ds(8, slots)], send.at[SB, n], recv.at[B, n], place(y, far, zh, x, core))

    def average(n):
        taken(pool.at[n, pl.ds(8, slots)], recv.at[B, n])
        mates = [mate_ref[k] for k in range(8)]

        def part(i, _):
            v = i // 5
            rows = pl.ds(pl.multiple_of((i % 5) * 16, 16), 16)
            held = [pool[n, j, v, rows, :] for j in range(8 + slots)]
            for k in range(8):
                value = held[0]
                for j in range(1, 8 + slots):
                    value = jnp.where(mates[k] == j, held[j], value)
                means[n, k, v, rows, :] = ((held[k].astype(F32) + value.astype(F32)) * 0.5).astype(BF16)
            return 0

        lax.fori_loop(0, 10, part, 0)
        for step in range(4):
            to_y = (y + step) % 4
            src, dst = means.at[n, (zl % 2) * 4 + to_y], pair.at[n, y]
            if step:
                remote(src, dst, send.at[SC, n], recv.at[C, n], place(to_y, zl, zh, x, core))
            else:
                pltpu.make_async_copy(src, dst, recv.at[C, n]).start()
            remote(
                means.at[n, (edge % 2) * 4 + to_y],
                dst,
                send.at[SC, n],
                recv.at[C, n],
                place(to_y, edge, zh, x, core),
            )

    def pass_on(n, rows, rsem, device):
        block = weights.at[n, rows]
        remote(block, block, send.at[SW, n], recv.at[rsem, n], device)

    def update(n):
        taken(pair.at[n], recv.at[C, n])
        moment_load(n).wait()

        def group(g, _):
            rows = pl.ds(pl.multiple_of(g * GROUP, 16), GROUP)
            own = outer[n, rows, :]
            delta = pair[n, g, 0].astype(F32)
            velocity = momentum_rate * moment[n, rows, :].astype(F32) + delta
            updated = (
                own
                - outer_rate * (delta + momentum_rate * velocity)
                - gossip_rate * (own - pair[n, g, 1].astype(F32))
            )
            outer[n, rows, :] = updated
            moment[n, rows, :] = velocity.astype(BF16)
            weights[n, pl.ds(pl.multiple_of(s * ROWS + g * GROUP, 16), GROUP), :] = updated.astype(BF16)
            return 0

        lax.fori_loop(0, 4, group, 0)
        own_rows = rows_of(zh, x, core)
        pass_on(n, own_rows, D, to_far)
        pass_on(n, own_rows, X1, to_right)
        pass_on(n, own_rows, X1, to_left)
        pass_on(n, own_rows, K, to_core)
        outer_store(n).start()
        moment_store(n).start()

    def outer_store(n):
        return pltpu.make_async_copy(outer.at[n], new_outer_hbm.at[:, cols(n)], local.at[OO, n])

    def moment_store(n):
        return pltpu.make_async_copy(moment.at[n], new_moment_hbm.at[:, cols(n)], local.at[OM, n])

    def kv_store(n):
        return pltpu.make_async_copy(kv.at[n], kv_hbm.at[:, cols(n)], local.at[OK, n])

    def forward(n, ph, rsem):
        pass_on(n, rows_of(ph, left, core, 0, HALF), rsem, to_right)
        pass_on(n, rows_of(ph, right, core, HALF, HALF), rsem, to_left)
        pass_on(n, rows_of(ph, left, core), K, to_core)
        pass_on(n, rows_of(ph, right, core), K, to_core)

    def first_hop(n):
        taken(weights.at[n, rows_of(1 - zh, x, core)], recv.at[D, n])
        far_rows = rows_of(1 - zh, x, core)
        pass_on(n, far_rows, X2, to_right)
        pass_on(n, far_rows, X2, to_left)
        pass_on(n, far_rows, K, to_core)
        taken(weights.at[n, pl.ds(0, 2 * ROWS)], recv.at[X1, n])
        forward(n, zh, F1)

    def second_hop(n):
        taken(weights.at[n, pl.ds(0, 2 * ROWS)], recv.at[X2, n])
        forward(n, 1 - zh, F2)
        taken(weights.at[n, pl.ds(0, ROWS)], recv.at[F1, n])
        pass_on(n, rows_of(zh, (x + 2) % 4, core), K, to_core)

    def third_hop(n):
        taken(weights.at[n, pl.ds(0, ROWS)], recv.at[F2, n])
        pass_on(n, rows_of(1 - zh, (x + 2) % 4, core), K, to_core)

    def norm_rows(t):
        @pl.when(t == 0)
        def _():
            token_load.wait()
            for copy in small_loads:
                copy.wait()
            turns = turn_ref[...]
            swapped = pltpu.roll(turns, HEAD_DIM // 2, 1)
            first = lax.broadcasted_iota(jnp.int32, turns.shape, 1) < HEAD_DIM // 2
            cos_ref[...] = jnp.where(first, turns, swapped)
            sin_ref[...] = jnp.where(first, -swapped, turns)

        per_tick = TOKENS // NORM_TICKS

        def part(i, _):
            rows = pl.ds(pl.multiple_of(t * per_tick + i * 16, 16), 16)
            values = normed[rows, :].astype(F32)
            mean_square = jnp.mean(values * values, axis=-1, keepdims=True)
            normed[rows, :] = (values * lax.rsqrt(mean_square + norm_eps) * gain_ref[...]).astype(BF16)
            return 0

        lax.fori_loop(0, per_tick // 16, part, 0)

    def project(n):
        taken(weights.at[n, pl.ds(0, DEPTH // 2)], recv.at[K, n])
        out = jnp.dot(normed[...], weights[n], preferred_element_type=F32) + bias_ref[:, cols(n)]

        @pl.when(n * CW < KEY_WIDTH)
        def _():
            for h in range(CW // HEAD_DIM):
                head = out[:, h * HEAD_DIM : (h + 1) * HEAD_DIM]
                turned = head * cos_ref[...] + pltpu.roll(head, HEAD_DIM // 2, 1) * sin_ref[...]
                kv[n, :, h * HEAD_DIM : (h + 1) * HEAD_DIM] = turned.astype(BF16)

        @pl.when(n * CW >= KEY_WIDTH)
        def _():
            kv[n] = out.astype(BF16)

        kv_store(n).start()

    def find_mates():
        found = [match_ref[p] for p in range(16)]

        def mate_of(on_side, k):
            replica = (k % 4) * 4 + on_side * 2 + k // 4
            mate = 0
            for p in range(16):
                mate = mate + jnp.where(found[p] == replica, found[p ^ 1], 0)
            crosses = jnp.where((mate // 2) % 2 != on_side, 1, 0)
            return (mate % 2) * 4 + mate // 4, crosses

        def ranks(crosses):
            return [sum(crosses[:k], 0) for k in range(8)]

        mates, crosses = zip(*[mate_of(side, k) for k in range(8)])
        if slots == 8:
            for k in range(8):
                mate_ref[k] = mates[k] + 8 * crosses[k]
            return
        rank = ranks(crosses)
        far_rank = ranks([mate_of(1 - side, k)[1] for k in range(8)])
        for k in range(8):
            place_far = 8
            for j in range(8):
                place_far = place_far + jnp.where(mates[k] == j, far_rank[j], 0)
            mate_ref[k] = jnp.where(crosses[k] == 1, place_far, mates[k])
        for slot in range(slots):
            which = 0
            for k in range(8):
                which = which + jnp.where(jnp.logical_and(crosses[k] == 1, rank[k] == slot), k, 0)
            mate_ref[8 + slot] = which

    def first_rows(n, _):
        send_rows(n)
        return 0

    lax.fori_loop(0, AHEAD, first_rows, 0)

    @pl.when(is_hub)
    def _():
        find_mates()

    if not DIRECT:

        @pl.when(jnp.logical_not(is_hub))
        def _():
            for n in range(EDGE_AHEAD):
                to_hub(n)

    def tick(t, _):
        if not DIRECT:

            @pl.when(jnp.logical_and(jnp.logical_not(is_hub), t + EDGE_AHEAD < CHUNKS))
            def _():
                to_hub(t + EDGE_AHEAD)

        def staged(lag, stage, also=None):
            ready = jnp.logical_and(t >= lag, t < CHUNKS + lag)

            @pl.when(ready if also is None else jnp.logical_and(ready, also))
            def _():
                stage(t - lag)

        @pl.when(jnp.logical_and(is_hub, t < CHUNKS))
        def _():
            swap_sides(t)

        staged(LAGS[0], average, is_hub)
        staged(LAGS[1], update)
        @pl.when(t + AHEAD < CHUNKS)
        def _():
            send_rows(t + AHEAD)

        staged(LAGS[2], first_hop)
        staged(LAGS[3], second_hop)
        staged(LAGS[4], third_hop)
        @pl.when(t < NORM_TICKS)
        def _():
            norm_rows(t)

        staged(LAGS[5], project)
        return 0

    lax.fori_loop(0, CHUNKS + LAGS[5], tick, 0)

    def drain(n, _):
        @pl.when(is_hub)
        def _():
            taken(sent.at[n, pl.ds(0, 3)], send.at[SA, n])
            taken(pool.at[n, pl.ds(8, slots)], send.at[SB, n])
            taken(means.at[n, pl.ds(0, 7)], send.at[SC, n])

        @pl.when(jnp.logical_not(is_hub))
        def _():
            if DIRECT:
                taken(sent.at[n], send.at[SA, n])
            else:
                taken(sent.at[n, pl.ds(0, 3)], send.at[SA, n])
                taken(pool.at[n, own_items], send.at[SE, n])

        taken(weights.at[n, pl.ds(0, 15 * ROWS)], send.at[SW, n])
        outer_store(n).wait()
        moment_store(n).wait()
        kv_store(n).wait()
        return 0

    lax.fori_loop(0, CHUNKS, drain, 0)


def turn_table(tokens):
    exponents = np.arange(HEAD_DIM // 2, dtype=np.float32) * np.float32(2.0 / HEAD_DIM)
    inverse = (rope_base ** (-exponents.astype(np.float64))).astype(np.float32)
    angles = np.arange(tokens, dtype=np.float32)[:, None] * inverse[None, :]
    angles = angles.astype(np.float64)
    return np.concatenate([np.cos(angles), np.sin(angles)], axis=1).astype(np.float32)


def launch(slots, *operands):
    hbm = pl.BlockSpec(memory_space=pl.ANY)
    smem = pl.BlockSpec(memory_space=pltpu.SMEM)
    return pl.pallas_call(
        functools.partial(kernel, slots),
        out_shape=(
            jax.ShapeDtypeStruct((ROWS, WIDTH), F32),
            jax.ShapeDtypeStruct((ROWS, WIDTH), BF16),
            jax.ShapeDtypeStruct((TOKENS, WIDTH), BF16),
        ),
        in_specs=[smem] + [hbm] * 7,
        out_specs=(hbm, hbm, hbm),
        scratch_shapes=[
            pltpu.VMEM((CHUNKS, ROWS, CW), F32),
            pltpu.VMEM((CHUNKS, ROWS, CW), BF16),
            pltpu.VMEM((CHUNKS, ROWS, CW), BF16),
            pltpu.VMEM((TOKENS, DEPTH), BF16),
            pltpu.VMEM((CHUNKS, 4, 2, GROUP, CW), BF16),
            pltpu.VMEM((CHUNKS, 8 + slots, 2, GROUP, CW), BF16),
            pltpu.VMEM((CHUNKS if slots < 8 else 1, slots, 2, GROUP, CW), BF16),
            pltpu.VMEM((CHUNKS, 8, 2, GROUP, CW), BF16),
            pltpu.VMEM((CHUNKS, 4, 2, GROUP, CW), BF16),
            pltpu.VMEM((CHUNKS, DEPTH, CW), BF16),
            pltpu.VMEM((CHUNKS, TOKENS, CW), BF16),
            pltpu.VMEM((1, DEPTH), F32),
            pltpu.VMEM((1, WIDTH), F32),
            pltpu.VMEM((TOKENS, HEAD_DIM), F32),
            pltpu.VMEM((TOKENS, HEAD_DIM), F32),
            pltpu.VMEM((TOKENS, HEAD_DIM), F32),
            pltpu.SMEM((16,), jnp.int32),
            pltpu.SemaphoreType.DMA((10, CHUNKS)),
            pltpu.SemaphoreType.DMA((5, CHUNKS)),
            pltpu.SemaphoreType.DMA((5, CHUNKS)),
            pltpu.SemaphoreType.DMA((4,)),
        ],
        compiler_params=pltpu.CompilerParams(
            collective_id=slots, has_side_effects=True, vmem_limit_bytes=62 * 2**20
        ),
    )(*operands)


def copy_kernel(*refs):
    sems = refs[-1]
    loads, stores = [], []
    for src, dst, held, parts in zip(refs[:3], refs[3:6], refs[6:9], (8, 4, 4)):
        size = src.shape[0] // parts
        for i in range(parts):
            rows, j = pl.ds(i * size, size), len(loads)
            loads.append(pltpu.make_async_copy(src.at[rows], held.at[rows], sems.at[0, j]))
            stores.append(pltpu.make_async_copy(held.at[rows], dst.at[rows], sems.at[1, j]))
    for load in loads:
        load.start()
    for load, store in zip(loads, stores):
        load.wait()
        store.start()
    for store in stores:
        store.wait()


def copied(*arrays):
    hbm = pl.BlockSpec(memory_space=pl.ANY)
    return pl.pallas_call(
        copy_kernel,
        out_shape=tuple(jax.ShapeDtypeStruct(a.shape, a.dtype) for a in arrays),
        in_specs=[hbm] * 3,
        out_specs=(hbm,) * 3,
        scratch_shapes=[pltpu.VMEM(a.shape, a.dtype) for a in arrays] + [pltpu.SemaphoreType.DMA((2, 16))],
        compiler_params=pltpu.CompilerParams(vmem_limit_bytes=16 * 2**20),
    )(*arrays)


def on_device(outer_weight, inner_weight, momentum, matching, tokens, norm_gain, kv_bias):
    order = jnp.arange(16, dtype=jnp.int32)
    paired = (order[None, :] == order[:, None] + 1) & (order[:, None] % 2 == 0)
    count = jnp.sum(jnp.where(paired, ((matching[None, :] ^ matching[:, None]) >> 1) & 1, 0))
    turns = jnp.asarray(turn_table(TOKENS * lax.axis_size("shard")))

    new_outer, new_moment, kv = lax.switch(
        jnp.clip((count - 3) // 2, 0, 2),
        [functools.partial(launch, slots) for slots in (4, 6, 8)],
        matching,
        outer_weight[0],
        inner_weight[0],
        momentum[0],
        tokens[0],
        norm_gain,
        kv_bias,
        turns,
    )
    new_outer, new_moment, kv = copied(new_outer, new_moment, kv)
    return (new_outer[None], new_moment[None], kv[None])


def solution(mesh):
    in_specs = (
        P("replica", "shard", None),
        P("replica", "shard", None),
        P("replica", "shard", None),
        P(),
        P("replica", "shard", None),
        P("replica", None),
        P("replica", None),
    )
    out_specs = (
        P("replica", "shard", None),
        P("replica", "shard", None),
        P("replica", "shard", None),
    )
    return jax.shard_map(on_device, mesh=mesh, in_specs=in_specs, out_specs=out_specs, check_vma=False)
```
